256 devices in a mesh: seq: 64 (over y, z, core), head: 4 (over x).
Axes of the slice: x: 4, y: 4, z: 8, core: 2. Of those that a mesh axis runs over, the one named last changes fastest.
Arguments:
- inputs: bfloat16 [32768, 4096], P('seq', 'head'), may hold values from -6 to 6
- rows_b: bfloat16 [32768, 128], P('seq'), may hold values from -6 to 6
- rows_c: bfloat16 [32768, 128], P('seq'), may hold values from -0.5 to 0.5
- log_decay: float32 [64, 32768], P('head', 'seq'), may hold values from -1 to 0, as said below
- score_cotangent: bfloat16 [32768, 2048], P('seq', 'head'), may hold values from -6 to 6
- out_weight: bfloat16 [4096, 2048], P('head'), may hold values from -0.09375 to 0.09375
Outputs:
- critic_hidden: bfloat16 [32768, 2048], P('seq', 'head')
- input_grad: bfloat16 [32768, 4096], P('seq', 'head')
- score_grad: bfloat16 [32768, 2048], P('seq', 'head')
The draws below stay inside these ranges and needn't reach their ends.
Inputs may be any that keep to these rules, and one draw needn't show every extreme that they name: `log_decay`: every entry is below zero.
All inputs are finite; a program needn't handle non-finite values.
Results may differ from the reference program's by a relative error of at most 0.025.
Values may be sent and summed in bfloat16 or wider, within the bound.
A program may use at most 192 MiB of HBM per device.

```python
import math
import jax
import jax.numpy as jnp
from jax import lax

D = 2048
ATTENTION_SPLITS = 64
P_SIZE = 64
N = 128
HP = 4096
Q = 256
F_DEV = 512
SEQUENCE_LENGTH = 32768
N_HEAD = 4


def draw_log_decay(key, part):
    stochastic_seed_parts = jax.random.split(key, 7)
    fast_share = 0.5
    fast_mask = jax.random.uniform(stochastic_seed_parts[0], (ATTENTION_SPLITS,)) < fast_share
    fast_rate = jnp.exp(jax.random.uniform(stochastic_seed_parts[1], (ATTENTION_SPLITS,), minval=math.log(1.0 / 50.0), maxval=math.log(1.0 / 30.0)))
    slow_rate = jnp.exp(jax.random.uniform(stochastic_seed_parts[2], (ATTENTION_SPLITS,), minval=math.log(0.15), maxval=math.log(0.4))) / SEQUENCE_LENGTH
    head_rate = jnp.where(fast_mask, fast_rate, slow_rate)
    block_factor = jnp.exp(jax.random.uniform(stochastic_seed_parts[3], (ATTENTION_SPLITS, SEQUENCE_LENGTH // F_DEV, 1), minval=math.log(0.5), maxval=math.log(2.0)))
    block_factor = (block_factor * jnp.ones((1, 1, F_DEV), jnp.float32)).reshape(ATTENTION_SPLITS, SEQUENCE_LENGTH)
    frame_factor = jnp.exp(jax.random.uniform(stochastic_seed_parts[4], (ATTENTION_SPLITS, SEQUENCE_LENGTH), minval=math.log(0.5), maxval=math.log(2.0)))
    timestep_decay_speeds = head_rate[:, None] * block_factor * frame_factor
    spike_locations = jax.random.randint(stochastic_seed_parts[5], (ATTENTION_SPLITS, 2), 0, SEQUENCE_LENGTH)
    objective_terms = jax.random.uniform(stochastic_seed_parts[6], (ATTENTION_SPLITS, 2), minval=math.log(1.25), maxval=math.log(2.0))
    spike_hit_flags = (jnp.arange(SEQUENCE_LENGTH)[None, :, None] == spike_locations[:, None, :]).astype(jnp.float32)
    spike_occurrences = jnp.sum(spike_hit_flags * objective_terms[:, None, :], axis=2)
    return (-(timestep_decay_speeds + spike_occurrences)).astype(jnp.float32)


def block_levels(rng, extent, shards, least, top_value):
    loudness, own = 1.0, jax.random.fold_in(rng, 6)
    for dim, parts in shards:
        draws = jnp.exp(jax.random.uniform(jax.random.fold_in(own, dim), (parts,), jnp.float32, least / len(shards), top_value / len(shards)))
        loudness = loudness * jnp.repeat(draws, extent[dim] // parts).reshape([-1 if axis == dim else 1 for axis in range(len(extent))])
    return loudness


def normal_values(key, dims, width, limit, cuts=(), held_as=jnp.bfloat16):
    drawn = width * jax.random.normal(key, dims, jnp.float32)
    if cuts:
        drawn = drawn * block_levels(key, dims, cuts, -0.22, 0.18)
    return jnp.clip(drawn, -limit, limit).astype(held_as)


def setup_inputs(seed: int = 0) -> dict:
    key_list = jax.random.split(jax.random.key(seed), 7)
    return {
        "inputs": normal_values(key_list[0], (SEQUENCE_LENGTH, HP), 1.0, 6.0, ((0, 64), (1, 4))),
        "rows_b": normal_values(key_list[1], (SEQUENCE_LENGTH, N), 1.0, 6.0, ((0, 64),)),
        "rows_c": normal_values(key_list[2], (SEQUENCE_LENGTH, N), N ** -0.5, 0.5, ((0, 64),)),
        "log_decay": draw_log_decay(jax.random.fold_in(key_list[6], 71), 0),
        "score_cotangent": normal_values(key_list[4], (SEQUENCE_LENGTH, D), 1.0, 6.0, ((0, 64), (1, 4))),
        "out_weight": normal_values(key_list[5], (HP, D), HP ** -0.5, 0.09375, ((0, 4),)),
    }


highest = lax.Precision.HIGHEST

def decay_tables(log_rates):
    cumulative = jnp.cumsum(log_rates, axis=1)
    spread = cumulative[:, :, None] - cumulative[:, None, :]
    length = log_rates.shape[1]
    lower_mask = (jnp.arange(length)[:, None] >= jnp.arange(length)[None, :])[None]
    within = jnp.where(lower_mask, jnp.exp(jnp.where(lower_mask, spread, 0.0)), 0.0)
    weight = jnp.sqrt(-jnp.expm1(2.0 * log_rates))
    return (cumulative, within, weight)

def prepare(rows_b, rows_c, log_rates):
    cumulative, within, weight = decay_tables(log_rates)
    scores = jnp.dot(rows_c, rows_b.T, preferred_element_type=jnp.float32)
    return (cumulative, within, weight, scores, rows_b.astype(jnp.float32), rows_c.astype(jnp.float32))

def block_forward(values, prepared, carry_state):
    cumulative, within, weight, scores, b_float, c_float = prepared
    head_count = cumulative.shape[0]
    frames = values.shape[0]
    driven = values.astype(jnp.float32).reshape(frames, head_count, -1) * weight.T[:, :, None]
    mixing = within * scores[None]
    intra_part = jnp.einsum('hts,shp->thp', mixing, driven, precision=highest)
    carried = jnp.exp(cumulative).T[:, :, None] * jnp.einsum('tn,hnp->thp', c_float, carry_state, precision=highest)
    tail_decay = jnp.exp(cumulative[:, -1:] - cumulative)
    new_state = jnp.exp(cumulative[:, -1])[:, None, None] * carry_state + jnp.einsum('sn,hs,shp->hnp', b_float, tail_decay, driven, precision=highest)
    return ((intra_part + carried).reshape(frames, -1), new_state)

def block_reverse(values, prepared, carry_state):
    cumulative, within, weight, scores, b_float, c_float = prepared
    head_count = cumulative.shape[0]
    frames = values.shape[0]
    driven = values.astype(jnp.float32).reshape(frames, head_count, -1)
    mixing = within * scores[None]
    intra_part = jnp.einsum('hst,shp->thp', mixing, driven, precision=highest)
    tail_decay = jnp.exp(cumulative[:, -1:] - cumulative)
    carried = tail_decay.T[:, :, None] * jnp.einsum('tn,hnp->thp', b_float, carry_state, precision=highest)
    result = weight.T[:, :, None] * (intra_part + carried)
    new_state = jnp.exp(cumulative[:, -1])[:, None, None] * carry_state + jnp.einsum('sn,hs,shp->hnp', c_float, jnp.exp(cumulative), driven, precision=highest)
    return (result.reshape(frames, -1), new_state)

def run_operator(values, rows_b, rows_c, log_decay, backwards):
    frames = values.shape[0]
    block_count = frames // Q
    value_blocks = values.reshape(block_count, Q, -1)
    b_blocks = rows_b.reshape(block_count, Q, N)
    c_blocks = rows_c.reshape(block_count, Q, N)
    log_blocks = log_decay.reshape(ATTENTION_SPLITS, block_count, Q).transpose(1, 0, 2)

    def stepper(carry_state, pieces):
        prepared = prepare(pieces[1], pieces[2], pieces[3])
        if backwards:
            output, carry_state = block_reverse(pieces[0], prepared, carry_state)
        else:
            output, carry_state = block_forward(pieces[0], prepared, carry_state)
        return (carry_state, output)
    zero_state = jnp.zeros((ATTENTION_SPLITS, N, P_SIZE), jnp.float32)
    _, outputs = lax.scan(stepper, zero_state, (value_blocks, b_blocks, c_blocks, log_blocks), reverse=backwards)
    return outputs.reshape(frames, -1)

def head_project(rows, out_weight):
    group_width = HP // N_HEAD
    accum_total = jnp.zeros((rows.shape[0], out_weight.shape[1]), jnp.float32)
    for group_index in range(N_HEAD):
        lo_edge = group_index * group_width
        partial_value = jnp.dot(rows[:, lo_edge:lo_edge + group_width], out_weight[lo_edge:lo_edge + group_width], preferred_element_type=jnp.float32)
        partial_value = lax.optimization_barrier(partial_value.astype(jnp.bfloat16)).astype(jnp.float32)
        accum_total = accum_total + partial_value
    return accum_total.astype(jnp.bfloat16)

def reference(inputs, rows_b, rows_c, log_decay, score_cotangent, out_weight):
    mixed = run_operator(inputs, rows_b, rows_c, log_decay, False).astype(jnp.bfloat16)
    critic_hidden = head_project(mixed, out_weight)
    pulled = jnp.dot(score_cotangent, out_weight.T, preferred_element_type=jnp.float32).astype(jnp.bfloat16)
    input_grad = run_operator(pulled, rows_b, rows_c, log_decay, True).astype(jnp.bfloat16)
    tangent = (2.0 * run_operator(input_grad, rows_b, rows_c, log_decay, False)).astype(jnp.bfloat16)
    score_grad = head_project(tangent, out_weight)
    return (critic_hidden, input_grad, score_grad)
```

```python
import functools

import jax
import jax.numpy as jnp
from jax import lax
from jax.experimental import pallas as pl
from jax.experimental.pallas import tpu as pltpu
from jax.sharding import PartitionSpec as P

Q = 256
F32 = jnp.float32
BF = jnp.bfloat16
MESH = pl.DeviceIdType.MESH
CHIPS = 32
LO, HI = slice(0, Q), slice(Q, 2 * Q)


def mm(a, b):
    return jnp.dot(a, b, preferred_element_type=F32)


def mm_nt(a, b):
    return lax.dot_general(a, b, (((1,), (1,)), ((), ())), preferred_element_type=F32)


def kernel(
    x_ref, b_ref, c_ref, ld_ref, sc_ref, w_hbm,
    ch_ref, ig_ref, sg_ref,
    w_v, rise_x, tw_x, bT, cT, cum, g_row, cumT, gT, sco, scoT, mix, mixT, dec,
    yl, vl, mid, end, sin, pulled, mixed, gbuf,
    ep_src, ep_dst, tot, rbuf, pbuf, sbuf, sp_src, sp_dst, dt, dtp, dchip, dall,
    pblk, ropp, from_l, from_r,
    w_sem, ag_s, ag_r, ex_s, ex_r, d_s, d_r, rs_s, rs_r,
):
    s_idx, hx = lax.axis_index("seq"), lax.axis_index("head")
    chip, core = s_idx // 2, lax.rem(s_idx, 2)
    right, left, opp = lax.rem(hx + 1, 4), lax.rem(hx + 3, 4), lax.rem(hx + 2, 4)
    dev_r, dev_l = (s_idx, right), (s_idx, left)
    dev_p = (2 * chip + 1 - core, hx)

    def rcopy(src, dst, ssem, rsem, dev):
        return pltpu.make_async_remote_copy(
            src_ref=src, dst_ref=dst, send_sem=ssem, recv_sem=rsem,
            device_id=dev, device_id_type=MESH,
        )

    barrier = pltpu.get_barrier_semaphore()
    for dev in (dev_r, dev_l, dev_p):
        pl.semaphore_signal(barrier, inc=1, device_id=dev, device_id_type=MESH)

    def greet(o, carry):
        d = lax.rem(chip + o, CHIPS)
        pl.semaphore_signal(barrier, inc=1, device_id=(2 * d + core, hx), device_id_type=MESH)
        return carry

    lax.fori_loop(1, CHIPS, greet, 0)
    w_copy = pltpu.make_async_copy(w_hbm, w_v, w_sem)
    w_copy.start()
    pl.semaphore_wait(barrier, 3 + CHIPS - 1)

    ag = [
        rcopy(sc_ref.at[LO], gbuf.at[hx, LO], ag_s.at[0], ag_r.at[0], dev_r),
        rcopy(sc_ref.at[HI], gbuf.at[hx, HI], ag_s.at[1], ag_r.at[1], dev_l),
        rcopy(sc_ref.at[HI], gbuf.at[hx, HI], ag_s.at[2], ag_r.at[2], dev_r),
        rcopy(sc_ref.at[LO], gbuf.at[hx, LO], ag_s.at[3], ag_r.at[3], dev_l),
        rcopy(gbuf.at[left, LO], gbuf.at[left, LO], ag_s.at[4], ag_r.at[4], dev_r),
        rcopy(gbuf.at[right, HI], gbuf.at[right, HI], ag_s.at[5], ag_r.at[5], dev_l),
    ]
    for copy in ag[:4]:
        copy.start()

    spread = (
        lax.broadcasted_iota(jnp.int32, (16, 1024), 0)
        == lax.shift_right_logical(lax.broadcasted_iota(jnp.int32, (16, 1024), 1), 6)
    ).astype(F32)
    spread_b = spread.astype(BF)
    lane = lax.broadcasted_iota(jnp.int32, (16, Q), 1)
    for blk in range(2):
        at = slice(blk * Q, (blk + 1) * Q)
        ld = ld_ref[:, at]
        y = -2.0 * ld
        series = jnp.ones_like(y)
        for k in range(9, 1, -1):
            series = 1.0 - y * (1.0 / k) * series
        log_w = 0.5 * jnp.log(jnp.where(y < 0.5, y * series, 1.0 - jnp.exp(-y)))
        c = ld
        for k in (1, 2, 4, 8, 16, 32, 64, 128):
            c = c + jnp.where(lane >= k, pltpu.roll(c, k, 1), 0.0)
        total = c[:, Q - 1 : Q]
        g = c - log_w
        cum[:, at] = c
        g_row[:, at] = g
        cumT[at, :] = c.T
        gT[at, :] = g.T
        rise_x[at, :] = mm(jnp.exp(c).T.astype(BF), spread_b).astype(BF)
        tw_x[at, :] = mm(jnp.exp(total - g).T.astype(BF), spread_b).astype(BF)
        dec[blk : blk + 1, :] = jnp.sum(spread * jnp.exp(total), axis=0, keepdims=True)
    d_dev = dec[0:1, :] * dec[1:2, :]
    dec[2:3, :] = d_dev
    for r in range(8):
        dt[r : r + 1, :] = d_dev[:, 128 * r : 128 * r + 128]
    bT[...] = b_ref[...].astype(F32).T.astype(BF)
    cT[...] = c_ref[...].astype(F32).T.astype(BF)
    low = lax.broadcasted_iota(jnp.int32, (Q, Q), 0) >= lax.broadcasted_iota(jnp.int32, (Q, Q), 1)
    high = lax.broadcasted_iota(jnp.int32, (Q, Q), 0) <= lax.broadcasted_iota(jnp.int32, (Q, Q), 1)
    for blk in range(2):
        at = slice(blk * Q, (blk + 1) * Q)
        sco[blk] = jnp.where(low, mm(c_ref[at, :], bT[:, at]), 0.0)
        scoT[blk] = jnp.where(high, mm(b_ref[at, :], cT[:, at]), 0.0)

    def make_table(table, rows_f, cols_f, score):
        def body(g, carry):
            for i in range(2):
                h = 2 * g + i
                onehot = lax.broadcasted_iota(jnp.int32, (Q, 16), 1) == h
                for blk in range(2):
                    at = slice(blk * Q, (blk + 1) * Q)
                    col = jnp.sum(jnp.where(onehot, cols_f[at, :], 0.0), axis=1, keepdims=True)
                    row = rows_f[pl.ds(h, 1), at]
                    gap = col - row if table is mix else row - col
                    value = jnp.exp(jnp.minimum(gap, 0.0)) * score[blk]
                    table[g, blk, :, i * Q : (i + 1) * Q] = value.astype(BF)
            return carry

        lax.fori_loop(0, 8, body, 0)

    lane_a = (lax.broadcasted_iota(jnp.int32, (Q, 128), 1) < 64).astype(F32)
    mask_a, mask_b = lane_a.astype(BF), (1.0 - lane_a).astype(BF)

    def intra(src, table, out):
        def body(g, carry):
            cols = pl.ds(pl.multiple_of(g * 128, 128), 128)
            for blk in range(2):
                at = slice(blk * Q, (blk + 1) * Q)
                z = src[at, cols]
                both = jnp.concatenate([z * mask_a, z * mask_b], axis=0)
                out[at, cols] = mm(table[g, blk], both)
            return carry

        lax.fori_loop(0, 8, body, 0)

    def end_state(k, src, scale, mapT, fwd):
        def body(q, carry):
            cols = pl.ds(pl.multiple_of(q * 256, 256), 256)
            p0 = mm(mapT[:, LO], src[LO, cols] * scale[LO, cols])
            p1 = mm(mapT[:, HI], src[HI, cols] * scale[HI, cols])
            if fwd:
                mid[k, :, cols] = p0
                end[k, :, cols] = dec[1:2, cols] * p0 + p1
            else:
                mid[k, :, cols] = p1
                end[k, :, cols] = dec[0:1, cols] * p1 + p0
            return carry

        lax.fori_loop(0, 4, body, 0)

    def finish(k, rows, local, scale, out, fwd, factor=None):
        def body(q, carry):
            cols = pl.ds(pl.multiple_of(q * 256, 256), 256)
            s = sin[k, :, cols]
            if fwd:
                s0, s1 = s, mid[k, :, cols] + dec[0:1, cols] * s
            else:
                s1, s0 = s, mid[k, :, cols] + dec[1:2, cols] * s
            for at, state in ((LO, s0), (HI, s1)):
                value = local[at, cols] + scale[at, cols].astype(F32) * mm(
                    rows[at, :], state.astype(BF)
                )
                if factor is not None:
                    value = factor * value
                out[at, cols] = value.astype(BF)
            return carry

        lax.fori_loop(0, 4, body, 0)

    mine = pl.ds(pl.multiple_of(core * 512, 512), 512)
    other = pl.ds(pl.multiple_of((1 - core) * 512, 512), 512)
    core_f = core.astype(F32)
    decay_row = 4 * core + lax.rem(chip, 4)

    def spread_out(src, dst, ssem, rsem):
        def body(o, carry):
            d = lax.rem(chip + o, CHIPS)
            rcopy(src.at[d], dst.at[chip], ssem, rsem, (2 * d + core, hx)).start()
            return carry

        lax.fori_loop(1, CHIPS, body, 0)

    def all_of(src, dst, ssem, rsem):
        part = pl.ds(0, CHIPS - 1)
        return rcopy(src.at[part], dst.at[part], ssem, rsem, dev_p)

    waits = []

    def ex_pair(k):
        ep_src[k] = end[k, :, other].astype(BF)
        rcopy(ep_src.at[k], ep_dst.at[k], ex_s.at[k, 0], ex_r.at[k, 0], dev_p).start()
        if k == 0:
            rcopy(dt, dtp, d_s.at[0], d_r.at[0], dev_p).start()

    def ex_out(k, fwd):
        copy = rcopy(ep_src.at[k], ep_dst.at[k], ex_s.at[k, 0], ex_r.at[k, 0], dev_p)
        copy.wait_recv()
        waits.append(copy)
        if k == 0:
            copy = rcopy(dt, dtp, d_s.at[0], d_r.at[0], dev_p)
            copy.wait_recv()
            waits.append(copy)
            dchip[...] = dt[...] * dtp[...]
            for r in range(8):
                dec[3:4, 128 * r : 128 * r + 128] = dtp[r : r + 1, :]
            dall[pl.ds(chip, 1)] = dchip[...][None]

            def body(o, carry):
                d = lax.rem(chip + o, CHIPS)
                rcopy(dchip, dall.at[chip], d_s.at[1], d_r.at[1], (2 * d + core, hx)).start()
                return carry

            lax.fori_loop(1, CHIPS, body, 0)
        first = 1.0 - core_f if fwd else core_f
        d_me, d_p = dec[2:3, mine], dec[3:4, mine]
        value = (1.0 - first + first * d_p) * end[k, :, mine] + (
            first + (1.0 - first) * d_me
        ) * ep_dst[k].astype(F32)
        value = value.astype(BF)
        for i in range(8):
            for j in range(4):
                tot[k, 4 * i + j] = value[16 * i : 16 * i + 16, 128 * j : 128 * j + 128]
        rbuf[k, pl.ds(chip, 1)] = tot[k, pl.ds(chip, 1)]
        spread_out(tot.at[k], rbuf.at[k], ex_s.at[k, 1], ex_r.at[k, 1])

    def ex_back(k, fwd):
        copy = all_of(tot.at[k], rbuf.at[k], ex_s.at[k, 1], ex_r.at[k, 1])
        copy.wait_recv()
        waits.append(copy)
        if k == 0:
            part = pl.ds(0, CHIPS - 1)
            copy = rcopy(dall.at[part], dall.at[part], d_s.at[1], d_r.at[1], dev_p)
            copy.wait_recv()
            waits.append(copy)
        run = jnp.zeros((16, 128), F32)
        for e in range(CHIPS) if fwd else range(CHIPS - 1, -1, -1):
            pbuf[k, e] = run.astype(BF)
            run = run * dall[e, pl.ds(decay_row, 1), :] + rbuf[k, e].astype(F32)
        sbuf[k, pl.ds(chip, 1)] = pbuf[k, pl.ds(chip, 1)]
        spread_out(pbuf.at[k], sbuf.at[k], ex_s.at[k, 2], ex_r.at[k, 2])

    def ex_split(k, fwd):
        copy = all_of(pbuf.at[k], sbuf.at[k], ex_s.at[k, 2], ex_r.at[k, 2])
        copy.wait_recv()
        waits.append(copy)
        first = 1.0 - core_f if fwd else core_f
        for j in range(4):
            cols = pl.ds(pl.multiple_of(core * 512 + 128 * j, 128), 128)
            d_me, d_p = dec[2:3, cols], dec[3:4, cols]
            for i in range(8):
                at = slice(16 * i, 16 * i + 16)
                s = sbuf[k, 4 * i + j].astype(F32)
                theirs = (1.0 - first + first * d_me) * s + first * end[k, at, cols]
                sp_src[k, at, 128 * j : 128 * j + 128] = theirs.astype(BF)
                e_p = ep_dst[k, at, 128 * j : 128 * j + 128].astype(F32)
                sin[k, at, cols] = (first + (1.0 - first) * d_p) * s + (1.0 - first) * e_p
        rcopy(sp_src.at[k], sp_dst.at[k], ex_s.at[k, 3], ex_r.at[k, 3], dev_p).start()

    def ex_end(k):
        copy = rcopy(sp_src.at[k], sp_dst.at[k], ex_s.at[k, 3], ex_r.at[k, 3], dev_p)
        copy.wait_recv()
        waits.append(copy)
        sin[k, :, other] = sp_dst[k].astype(F32)

    def project(r, slot, dest):
        cols = pl.ds(pl.multiple_of(dest * 512, 512), 512)

        def body(i, carry):
            at = pl.ds(pl.multiple_of(i * Q, Q), Q)
            pblk[r, slot, at, :] = mm(mixed[at, :], w_v[:, cols]).astype(BF)
            return carry

        lax.fori_loop(0, 2, body, 0)

    def rs_copies(r):
        return [
            rcopy(pblk.at[r, 0, LO], ropp.at[r, 0], rs_s.at[r, 0], rs_r.at[r, 0], dev_r),
            rcopy(pblk.at[r, 0, HI], ropp.at[r, 1], rs_s.at[r, 1], rs_r.at[r, 1], dev_l),
            rcopy(pblk.at[r, 1, HI], from_l.at[r, HI], rs_s.at[r, 2], rs_r.at[r, 2], dev_r),
            rcopy(pblk.at[r, 2, LO], from_r.at[r, LO], rs_s.at[r, 3], rs_r.at[r, 3], dev_l),
            rcopy(pblk.at[r, 1, LO], from_l.at[r, LO], rs_s.at[r, 4], rs_r.at[r, 4], dev_r),
            rcopy(pblk.at[r, 2, HI], from_r.at[r, HI], rs_s.at[r, 5], rs_r.at[r, 5], dev_l),
        ]

    rs = [rs_copies(0), rs_copies(1)]

    def rs_first(r):
        project(r, 0, opp)
        rs[r][0].start()
        rs[r][1].start()

    def rs_second(r):
        project(r, 1, right)
        rs[r][2].start()
        project(r, 2, left)
        rs[r][3].start()
        project(r, 3, hx)

    def rs_mid(r):
        rs[r][0].wait_recv()
        pblk[r, 1, LO, :] = (pblk[r, 1, LO, :].astype(F32) + ropp[r, 0].astype(F32)).astype(BF)
        rs[r][4].start()
        rs[r][1].wait_recv()
        pblk[r, 2, HI, :] = (pblk[r, 2, HI, :].astype(F32) + ropp[r, 1].astype(F32)).astype(BF)
        rs[r][5].start()

    def rs_end(r, out):
        for copy in rs[r][2:]:
            copy.wait_recv()
        out[...] = (
            pblk[r, 3].astype(F32) + from_l[r].astype(F32) + from_r[r].astype(F32)
        ).astype(BF)

    def pull_first():
        def body(n, carry):
            rows = pl.ds(pl.multiple_of(n * Q, Q), Q)
            total = jnp.zeros((2 * Q, Q), F32)
            for block, dest in ((sc_ref, hx), (gbuf.at[left], left), (gbuf.at[right], right)):
                cols = pl.ds(pl.multiple_of(dest * 512, 512), 512)
                total = total + mm_nt(block[...], w_v[rows, cols])
            vl[:, rows] = total
            return carry

        lax.fori_loop(0, 4, body, 0)

    def pull_last():
        cols = pl.ds(pl.multiple_of(opp * 512, 512), 512)

        def body(n, carry):
            rows = pl.ds(pl.multiple_of(n * Q, Q), Q)
            pulled[:, rows] = (vl[:, rows] + mm_nt(gbuf[opp], w_v[rows, cols])).astype(BF)
            return carry

        lax.fori_loop(0, 4, body, 0)

    end_state(0, x_ref, tw_x, bT, True)
    ex_pair(0)
    make_table(mix, g_row, cumT, sco)
    ex_out(0, True)
    intra(x_ref, mix, yl)
    ex_back(0, True)
    make_table(mixT, cum, gT, scoT)
    ex_split(0, True)
    ag[0].wait_recv()
    ag[4].start()
    ag[1].wait_recv()
    ag[5].start()
    ag[2].wait_recv()
    ag[3].wait_recv()
    w_copy.wait()
    pull_first()
    ex_end(0)
    finish(0, c_ref, yl, rise_x, mixed, True)
    ag[4].wait_recv()
    ag[5].wait_recv()
    pull_last()
    end_state(1, pulled, rise_x, cT, False)
    ex_pair(1)
    rs_first(0)
    ex_out(1, False)
    rs_second(0)
    ex_back(1, False)
    intra(pulled, mixT, vl)
    ex_split(1, False)
    rs_mid(0)
    ex_end(1)
    finish(1, b_ref, vl, tw_x, ig_ref, False)
    end_state(2, ig_ref, tw_x, bT, True)
    ex_pair(2)
    intra(ig_ref, mix, yl)
    ex_out(2, True)
    rs_end(0, ch_ref)
    ex_back(2, True)
    ex_split(2, True)
    ex_end(2)
    finish(2, c_ref, yl, rise_x, mixed, True, 2.0)
    rs_first(1)
    rs_second(1)
    rs_mid(1)
    rs_end(1, sg_ref)
    for copy in waits + ag + rs[0] + rs[1]:
        copy.wait_send()


def local(inputs, rows_b, rows_c, log_decay, score_cotangent, out_weight):
    vm = pltpu.VMEM
    dma = pltpu.SemaphoreType.DMA
    scratch = [
        vm((1024, 2048), BF), vm((512, 1024), BF), vm((512, 1024), BF),
        vm((128, 512), BF), vm((128, 512), BF),
        vm((16, 512), F32), vm((16, 512), F32), vm((512, 16), F32), vm((512, 16), F32),
        vm((2, Q, Q), F32), vm((2, Q, Q), F32),
        vm((8, 2, Q, 2 * Q), BF), vm((8, 2, Q, 2 * Q), BF), vm((8, 1024), F32),
        vm((512, 1024), F32), vm((512, 1024), F32),
        vm((3, 128, 1024), F32), vm((3, 128, 1024), F32), vm((3, 128, 1024), F32),
        vm((512, 1024), BF), vm((512, 1024), BF), vm((4, 512, 512), BF),
        vm((3, 128, 512), BF), vm((3, 128, 512), BF),
        vm((3, CHIPS, 16, 128), BF), vm((3, CHIPS, 16, 128), BF),
        vm((3, CHIPS, 16, 128), BF), vm((3, CHIPS, 16, 128), BF),
        vm((3, 128, 512), BF), vm((3, 128, 512), BF),
        vm((8, 128), F32), vm((8, 128), F32), vm((8, 128), F32), vm((CHIPS, 8, 128), F32),
        vm((2, 4, 512, 512), BF), vm((2, 2, Q, 512), BF),
        vm((2, 512, 512), BF), vm((2, 512, 512), BF),
        dma, dma((6,)), dma((6,)), dma((3, 4)), dma((3, 4)), dma((2,)), dma((2,)),
        dma((2, 6)), dma((2, 6)),
    ]
    spec = pl.BlockSpec(memory_space=vm)
    return pl.pallas_call(
        kernel,
        out_shape=(
            jax.ShapeDtypeStruct((512, 512), BF),
            jax.ShapeDtypeStruct((512, 1024), BF),
            jax.ShapeDtypeStruct((512, 512), BF),
        ),
        in_specs=[spec] * 5 + [pl.BlockSpec(memory_space=pl.ANY)],
        out_specs=(spec, spec, spec),
        scratch_shapes=scratch,
        compiler_params=pltpu.CompilerParams(
            collective_id=0, has_side_effects=True, vmem_limit_bytes=58 * 1024 * 1024
        ),
        cost_estimate=pl.CostEstimate(flops=8 * 10**9, bytes_accessed=10**7, transcendentals=0),
    )(inputs, rows_b, rows_c, log_decay, score_cotangent, out_weight)


def solution(mesh):
    return jax.shard_map(
        local,
        mesh=mesh,
        in_specs=(
            P("seq", "head"),
            P("seq", None),
            P("seq", None),
            P("head", "seq"),
            P("seq", "head"),
            P("head", None),
        ),
        out_specs=(P("seq", "head"), P("seq", "head"), P("seq", "head")),
        check_vma=False,
    )
```

```python
import functools

import jax
import jax.numpy as jnp
from jax import lax
from jax.experimental import pallas as pl
from jax.experimental.pallas import tpu as pltpu
from jax.sharding import PartitionSpec as P

Q = 256
F32 = jnp.float32
BF = jnp.bfloat16
MESH = pl.DeviceIdType.MESH
CHIPS = 32
LO, HI = slice(0, Q), slice(Q, 2 * Q)


def mm(a, b):
    return jnp.dot(a, b, preferred_element_type=F32)


def mm_nt(a, b):
    return lax.dot_general(a, b, (((1,), (1,)), ((), ())), preferred_element_type=F32)


def kernel(
    x_hbm, b_hbm, c_hbm, ld_hbm, sc_hbm, w_hbm,
    ch_hbm, ig_hbm, sg_hbm,
    x_ref, b_ref, c_ref, ld_ref, sc_ref, ch_ref, ig_ref, sg_ref, w_v, rise_x, tw_x, bT, cT, cum, g_row, cumT, gT, sco, scoT, mix, mixT, dec,
    yl, vl, mid, end, sin, pulled, mixed, gbuf,
    ep_src, ep_dst, tot, rbuf, pbuf, sbuf, sp_src, sp_dst, dt, dtp, dchip, dall,
    pblk, ropp, from_l, from_r,
    in_sem, out_sem, round_sem, ag_s, ag_r, ex_s, ex_r, d_s, d_r, rs_s, rs_r,
):
    s_idx, hx = lax.axis_index("seq"), lax.axis_index("head")
    chip, core = s_idx // 2, lax.rem(s_idx, 2)
    right, left, opp = lax.rem(hx + 1, 4), lax.rem(hx + 3, 4), lax.rem(hx + 2, 4)
    dev_r, dev_l = (s_idx, right), (s_idx, left)
    dev_p = (2 * chip + 1 - core, hx)

    def rcopy(src, dst, ssem, rsem, dev):
        return pltpu.make_async_remote_copy(
            src_ref=src, dst_ref=dst, send_sem=ssem, recv_sem=rsem,
            device_id=dev, device_id_type=MESH,
        )

    y, z = chip // 8, lax.rem(chip, 8)

    def along_z(o):
        return (2 * (8 * y + lax.rem(z + o, 8)) + core, hx)

    def along_y(o):
        return (2 * (8 * lax.rem(y + o, 4) + z) + core, hx)

    barrier = pltpu.get_barrier_semaphore()
    for dev in (dev_r, dev_l, dev_p, along_z(1), along_z(7), along_y(1), along_y(3)):
        pl.semaphore_signal(barrier, inc=1, device_id=dev, device_id_type=MESH)
    loads = [
        pltpu.make_async_copy(src, dst, in_sem.at[i])
        for i, (src, dst) in enumerate(
            (
                (sc_hbm, sc_ref), (ld_hbm, ld_ref), (b_hbm, b_ref),
                (c_hbm, c_ref), (x_hbm, x_ref), (w_hbm, w_v),
            )
        )
    ]
    for copy in loads:
        copy.start()
    loads[0].wait()
    pl.semaphore_wait(barrier, 7)

    def tell(i, devs):
        for dev in devs:
            pl.semaphore_signal(round_sem.at[i], inc=1, device_id=dev, device_id_type=MESH)

    def heard(i):
        pl.semaphore_wait(round_sem.at[i], 2)

    ag = [
        rcopy(sc_ref.at[LO], gbuf.at[hx, LO], ag_s.at[0], ag_r.at[0], dev_r),
        rcopy(sc_ref.at[HI], gbuf.at[hx, HI], ag_s.at[1], ag_r.at[1], dev_l),
        rcopy(sc_ref.at[HI], gbuf.at[hx, HI], ag_s.at[2], ag_r.at[2], dev_r),
        rcopy(sc_ref.at[LO], gbuf.at[hx, LO], ag_s.at[3], ag_r.at[3], dev_l),
        rcopy(gbuf.at[left, LO], gbuf.at[left, LO], ag_s.at[4], ag_r.at[4], dev_r),
        rcopy(gbuf.at[right, HI], gbuf.at[right, HI], ag_s.at[5], ag_r.at[5], dev_l),
    ]
    for copy in ag[:4]:
        copy.start()
    tell(0, (along_z(1), along_z(7)))
    for copy in loads[1:4]:
        copy.wait()

    spread = (
        lax.broadcasted_iota(jnp.int32, (16, 1024), 0)
        == lax.shift_right_logical(lax.broadcasted_iota(jnp.int32, (16, 1024), 1), 6)
    ).astype(F32)
    spread_b = spread.astype(BF)
    lane = lax.broadcasted_iota(jnp.int32, (16, Q), 1)
    for blk in range(2):
        at = slice(blk * Q, (blk + 1) * Q)
        ld = ld_ref[:, at]
        u = -2.0 * ld
        series = jnp.ones_like(u)
        for k in range(9, 1, -1):
            series = 1.0 - u * (1.0 / k) * series
        log_w = 0.5 * jnp.log(jnp.where(u < 0.5, u * series, 1.0 - jnp.exp(-u)))
        c = ld
        for k in (1, 2, 4, 8, 16, 32, 64, 128):
            c = c + jnp.where(lane >= k, pltpu.roll(c, k, 1), 0.0)
        total = c[:, Q - 1 : Q]
        g = c - log_w
        cum[:, at] = c
        g_row[:, at] = g
        cumT[at, :] = c.T
        gT[at, :] = g.T
        rise_x[at, :] = mm(jnp.exp(c).T.astype(BF), spread_b).astype(BF)
        tw_x[at, :] = mm(jnp.exp(total - g).T.astype(BF), spread_b).astype(BF)
        dec[blk : blk + 1, :] = jnp.sum(spread * jnp.exp(total), axis=0, keepdims=True)
    heard(0)
    tell(1, (along_z(2), along_z(6)))
    d_dev = dec[0:1, :] * dec[1:2, :]
    dec[2:3, :] = d_dev
    for r in range(8):
        dt[r : r + 1, :] = d_dev[:, 128 * r : 128 * r + 128]
    bT[...] = b_ref[...].astype(F32).T.astype(BF)
    cT[...] = c_ref[...].astype(F32).T.astype(BF)
    low = lax.broadcasted_iota(jnp.int32, (Q, Q), 0) >= lax.broadcasted_iota(jnp.int32, (Q, Q), 1)
    high = lax.broadcasted_iota(jnp.int32, (Q, Q), 0) <= lax.broadcasted_iota(jnp.int32, (Q, Q), 1)
    for blk in range(2):
        at = slice(blk * Q, (blk + 1) * Q)
        sco[blk] = jnp.where(low, mm(c_ref[at, :], bT[:, at]), 0.0)
        scoT[blk] = jnp.where(high, mm(b_ref[at, :], cT[:, at]), 0.0)

    def make_table(table, rows_f, cols_f, score):
        def body(g, carry):
            for i in range(2):
                h = 2 * g + i
                onehot = lax.broadcasted_iota(jnp.int32, (Q, 16), 1) == h
                for blk in range(2):
                    at = slice(blk * Q, (blk + 1) * Q)
                    col = jnp.sum(jnp.where(onehot, cols_f[at, :], 0.0), axis=1, keepdims=True)
                    row = rows_f[pl.ds(h, 1), at]
                    gap = col - row if table is mix else row - col
                    value = jnp.exp(jnp.minimum(gap, 0.0)) * score[blk]
                    table[g, blk, :, i * Q : (i + 1) * Q] = value.astype(BF)
            return carry

        lax.fori_loop(0, 8, body, 0)

    lane_a = (lax.broadcasted_iota(jnp.int32, (Q, 128), 1) < 64).astype(F32)
    mask_a, mask_b = lane_a.astype(BF), (1.0 - lane_a).astype(BF)

    def intra(src, table, out):
        def body(g, carry):
            cols = pl.ds(pl.multiple_of(g * 128, 128), 128)
            for blk in range(2):
                at = slice(blk * Q, (blk + 1) * Q)
                z = src[at, cols]
                both = jnp.concatenate([z * mask_a, z * mask_b], axis=0)
                out[at, cols] = mm(table[g, blk], both)
            return carry

        lax.fori_loop(0, 8, body, 0)

    def end_state(k, src, scale, mapT, fwd):
        def body(q, carry):
            cols = pl.ds(pl.multiple_of(q * 256, 256), 256)
            p0 = mm(mapT[:, LO], src[LO, cols] * scale[LO, cols])
            p1 = mm(mapT[:, HI], src[HI, cols] * scale[HI, cols])
            if fwd:
                mid[k, :, cols] = p0
                end[k, :, cols] = dec[1:2, cols] * p0 + p1
            else:
                mid[k, :, cols] = p1
                end[k, :, cols] = dec[0:1, cols] * p1 + p0
            return carry

        lax.fori_loop(0, 4, body, 0)

    def finish(k, rows, local, scale, out, fwd, factor=None):
        def body(q, carry):
            cols = pl.ds(pl.multiple_of(q * 256, 256), 256)
            s = sin[k, :, cols]
            if fwd:
                s0, s1 = s, mid[k, :, cols] + dec[0:1, cols] * s
            else:
                s1, s0 = s, mid[k, :, cols] + dec[1:2, cols] * s
            for at, state in ((LO, s0), (HI, s1)):
                value = local[at, cols] + scale[at, cols].astype(F32) * mm(
                    rows[at, :], state.astype(BF)
                )
                if factor is not None:
                    value = factor * value
                out[at, cols] = value.astype(BF)
            return carry

        lax.fori_loop(0, 4, body, 0)

    mine = pl.ds(pl.multiple_of(core * 512, 512), 512)
    other = pl.ds(pl.multiple_of((1 - core) * 512, 512), 512)
    core_f = core.astype(F32)
    decay_row = 4 * core + lax.rem(chip, 4)

    def far_first(o):
        j, k = o // 8, lax.rem(o, 8)
        dz = 4 + (k // 2) - lax.rem(k, 2) * (k // 2 + (k + 1) // 2)
        dy = 2 + (j // 2) - lax.rem(j, 2) * (j // 2 + (j + 1) // 2)
        return 8 * lax.rem(y + dy, 4) + lax.rem(z + dz, 8)

    def spread_out(src, dst, ssem, rsem):
        def body(o, carry):
            d = far_first(o)
            rcopy(src.at[d], dst.at[chip], ssem, rsem, (2 * d + core, hx)).start()
            return carry

        lax.fori_loop(0, CHIPS - 1, body, 0)

    def all_of(src, dst, ssem, rsem):
        part = pl.ds(0, CHIPS - 1)
        return rcopy(src.at[part], dst.at[part], ssem, rsem, dev_p)

    waits = []

    def ex_pair(k):
        ep_src[k] = end[k, :, other].astype(BF)
        rcopy(ep_src.at[k], ep_dst.at[k], ex_s.at[k, 0], ex_r.at[k, 0], dev_p).start()
        if k == 0:
            rcopy(dt, dtp, d_s.at[0], d_r.at[0], dev_p).start()

    def ex_out(k, fwd):
        copy = rcopy(ep_src.at[k], ep_dst.at[k], ex_s.at[k, 0], ex_r.at[k, 0], dev_p)
        copy.wait_recv()
        waits.append(copy)
        if k == 0:
            copy = rcopy(dt, dtp, d_s.at[0], d_r.at[0], dev_p)
            copy.wait_recv()
            waits.append(copy)
            dchip[...] = dt[...] * dtp[...]
            for r in range(8):
                dec[3:4, 128 * r : 128 * r + 128] = dtp[r : r + 1, :]
            dall[pl.ds(chip, 1)] = dchip[...][None]

            def body(o, carry):
                d = far_first(o)
                rcopy(dchip, dall.at[chip], d_s.at[1], d_r.at[1], (2 * d + core, hx)).start()
                return carry

            lax.fori_loop(0, CHIPS - 1, body, 0)
        first = 1.0 - core_f if fwd else core_f
        d_me, d_p = dec[2:3, mine], dec[3:4, mine]
        value = (1.0 - first + first * d_p) * end[k, :, mine] + (
            first + (1.0 - first) * d_me
        ) * ep_dst[k].astype(F32)
        value = value.astype(BF)
        for i in range(8):
            for j in range(4):
                tot[k, 4 * i + j] = value[16 * i : 16 * i + 16, 128 * j : 128 * j + 128]
        rbuf[k, pl.ds(chip, 1)] = tot[k, pl.ds(chip, 1)]
        spread_out(tot.at[k], rbuf.at[k], ex_s.at[k, 1], ex_r.at[k, 1])

    def ex_back(k, fwd):
        copy = all_of(tot.at[k], rbuf.at[k], ex_s.at[k, 1], ex_r.at[k, 1])
        copy.wait_recv()
        waits.append(copy)
        if k == 0:
            part = pl.ds(0, CHIPS - 1)
            copy = rcopy(dall.at[part], dall.at[part], d_s.at[1], d_r.at[1], dev_p)
            copy.wait_recv()
            waits.append(copy)
        run = jnp.zeros((16, 128), F32)
        for e in range(CHIPS) if fwd else range(CHIPS - 1, -1, -1):
            pbuf[k, e] = run.astype(BF)
            run = run * dall[e, pl.ds(decay_row, 1), :] + rbuf[k, e].astype(F32)
        sbuf[k, pl.ds(chip, 1)] = pbuf[k, pl.ds(chip, 1)]
        spread_out(pbuf.at[k], sbuf.at[k], ex_s.at[k, 2], ex_r.at[k, 2])

    def ex_split(k, fwd):
        copy = all_of(pbuf.at[k], sbuf.at[k], ex_s.at[k, 2], ex_r.at[k, 2])
        copy.wait_recv()
        waits.append(copy)
        first = 1.0 - core_f if fwd else core_f
        for j in range(4):
            cols = pl.ds(pl.multiple_of(core * 512 + 128 * j, 128), 128)
            d_me, d_p = dec[2:3, cols], dec[3:4, cols]
            for i in range(8):
                at = slice(16 * i, 16 * i + 16)
                s = sbuf[k, 4 * i + j].astype(F32)
                theirs = (1.0 - first + first * d_me) * s + first * end[k, at, cols]
                sp_src[k, at, 128 * j : 128 * j + 128] = theirs.astype(BF)
                e_p = ep_dst[k, at, 128 * j : 128 * j + 128].astype(F32)
                sin[k, at, cols] = (first + (1.0 - first) * d_p) * s + (1.0 - first) * e_p
        rcopy(sp_src.at[k], sp_dst.at[k], ex_s.at[k, 3], ex_r.at[k, 3], dev_p).start()

    def ex_end(k):
        copy = rcopy(sp_src.at[k], sp_dst.at[k], ex_s.at[k, 3], ex_r.at[k, 3], dev_p)
        copy.wait_recv()
        waits.append(copy)
        sin[k, :, other] = sp_dst[k].astype(F32)

    def project(r, slot, dest, at):
        cols = pl.ds(pl.multiple_of(dest * 512, 512), 512)
        pblk[r, slot, at, :] = mm(mixed[at, :], w_v[:, cols]).astype(BF)

    def rs_copies(r):
        return [
            rcopy(pblk.at[r, 0, LO], ropp.at[r, 0], rs_s.at[r, 0], rs_r.at[r, 0], dev_r),
            rcopy(pblk.at[r, 0, HI], ropp.at[r, 1], rs_s.at[r, 1], rs_r.at[r, 1], dev_l),
            rcopy(pblk.at[r, 1, HI], from_l.at[r, HI], rs_s.at[r, 2], rs_r.at[r, 2], dev_r),
            rcopy(pblk.at[r, 2, LO], from_r.at[r, LO], rs_s.at[r, 3], rs_r.at[r, 3], dev_l),
            rcopy(pblk.at[r, 1, LO], from_l.at[r, LO], rs_s.at[r, 4], rs_r.at[r, 4], dev_r),
            rcopy(pblk.at[r, 2, HI], from_r.at[r, HI], rs_s.at[r, 5], rs_r.at[r, 5], dev_l),
        ]

    rs = [rs_copies(0), rs_copies(1)]

    def rs_first(r):
        project(r, 0, opp, LO)
        rs[r][0].start()
        project(r, 0, opp, HI)
        rs[r][1].start()

    def rs_second(r):
        project(r, 1, right, HI)
        rs[r][2].start()
        project(r, 2, left, LO)
        rs[r][3].start()
        project(r, 1, right, LO)
        project(r, 2, left, HI)
        project(r, 3, hx, LO)
        project(r, 3, hx, HI)

    def rs_mid(r):
        rs[r][0].wait_recv()
        pblk[r, 1, LO, :] = (pblk[r, 1, LO, :].astype(F32) + ropp[r, 0].astype(F32)).astype(BF)
        rs[r][4].start()
        rs[r][1].wait_recv()
        pblk[r, 2, HI, :] = (pblk[r, 2, HI, :].astype(F32) + ropp[r, 1].astype(F32)).astype(BF)
        rs[r][5].start()

    def rs_end(r, out):
        for copy in rs[r][2:]:
            copy.wait_recv()
        out[...] = (
            pblk[r, 3].astype(F32) + from_l[r].astype(F32) + from_r[r].astype(F32)
        ).astype(BF)

    def pull_first():
        def body(n, carry):
            rows = pl.ds(pl.multiple_of(n * Q, Q), Q)
            total = jnp.zeros((2 * Q, Q), F32)
            for block, dest in ((sc_ref, hx), (gbuf.at[left], left), (gbuf.at[right], right)):
                cols = pl.ds(pl.multiple_of(dest * 512, 512), 512)
                total = total + mm_nt(block[...], w_v[rows, cols])
            vl[:, rows] = total
            return carry

        lax.fori_loop(0, 4, body, 0)

    def pull_last():
        cols = pl.ds(pl.multiple_of(opp * 512, 512), 512)

        def body(n, carry):
            rows = pl.ds(pl.multiple_of(n * Q, Q), Q)
            pulled[:, rows] = (vl[:, rows] + mm_nt(gbuf[opp], w_v[rows, cols])).astype(BF)
            return carry

        lax.fori_loop(0, 4, body, 0)

    stores = [
        pltpu.make_async_copy(src, dst, out_sem.at[i])
        for i, (src, dst) in enumerate(((ch_ref, ch_hbm), (ig_ref, ig_hbm), (sg_ref, sg_hbm)))
    ]
    heard(1)
    tell(2, (along_y(1), along_y(3)))
    loads[4].wait()
    end_state(0, x_ref, tw_x, bT, True)
    ex_pair(0)
    heard(2)
    tell(3, (along_y(1), along_y(3)))
    make_table(mix, g_row, cumT, sco)
    heard(3)
    ex_out(0, True)
    intra(x_ref, mix, yl)
    ex_back(0, True)
    make_table(mixT, cum, gT, scoT)
    ex_split(0, True)
    ag[0].wait_recv()
    ag[4].start()
    ag[1].wait_recv()
    ag[5].start()
    ag[2].wait_recv()
    ag[3].wait_recv()
    loads[5].wait()
    pull_first()
    ex_end(0)
    finish(0, c_ref, yl, rise_x, mixed, True)
    ag[4].wait_recv()
    ag[5].wait_recv()
    pull_last()
    end_state(1, pulled, rise_x, cT, False)
    ex_pair(1)
    rs_first(0)
    ex_out(1, False)
    rs_second(0)
    ex_back(1, False)
    intra(pulled, mixT, vl)
    ex_split(1, False)
    rs_mid(0)
    ex_end(1)
    finish(1, b_ref, vl, tw_x, ig_ref, False)
    stores[1].start()
    end_state(2, ig_ref, tw_x, bT, True)
    ex_pair(2)
    intra(ig_ref, mix, yl)
    ex_out(2, True)
    rs_end(0, ch_ref)
    stores[0].start()
    ex_back(2, True)
    ex_split(2, True)
    ex_end(2)
    finish(2, c_ref, yl, rise_x, mixed, True, 2.0)
    rs_first(1)
    rs_second(1)
    rs_mid(1)
    rs_end(1, sg_ref)
    stores[2].start()
    for copy in waits + ag + rs[0] + rs[1]:
        copy.wait_send()
    for copy in stores:
        copy.wait()


def hand_on(*refs):
    sems = refs[6]
    copies = [pltpu.make_async_copy(refs[i], refs[3 + i], sems.at[i]) for i in range(3)]
    for copy in copies:
        copy.start()
    for copy in copies:
        copy.wait()


def local(inputs, rows_b, rows_c, log_decay, score_cotangent, out_weight):
    vm = pltpu.VMEM
    dma = pltpu.SemaphoreType.DMA
    scratch = [
        vm((512, 1024), BF), vm((512, 128), BF), vm((512, 128), BF), vm((16, 512), F32),
        vm((512, 512), BF), vm((512, 512), BF), vm((512, 1024), BF), vm((512, 512), BF),
        vm((1024, 2048), BF), vm((512, 1024), BF), vm((512, 1024), BF),
        vm((128, 512), BF), vm((128, 512), BF),
        vm((16, 512), F32), vm((16, 512), F32), vm((512, 16), F32), vm((512, 16), F32),
        vm((2, Q, Q), F32), vm((2, Q, Q), F32),
        vm((8, 2, Q, 2 * Q), BF), vm((8, 2, Q, 2 * Q), BF), vm((8, 1024), F32),
        vm((512, 1024), F32), vm((512, 1024), F32),
        vm((3, 128, 1024), F32), vm((3, 128, 1024), F32), vm((3, 128, 1024), F32),
        vm((512, 1024), BF), vm((512, 1024), BF), vm((4, 512, 512), BF),
        vm((3, 128, 512), BF), vm((3, 128, 512), BF),
        vm((3, CHIPS, 16, 128), BF), vm((3, CHIPS, 16, 128), BF),
        vm((3, CHIPS, 16, 128), BF), vm((3, CHIPS, 16, 128), BF),
        vm((3, 128, 512), BF), vm((3, 128, 512), BF),
        vm((8, 128), F32), vm((8, 128), F32), vm((8, 128), F32), vm((CHIPS, 8, 128), F32),
        vm((2, 4, 512, 512), BF), vm((2, 2, Q, 512), BF),
        vm((2, 512, 512), BF), vm((2, 512, 512), BF),
        dma((6,)), dma((3,)), pltpu.SemaphoreType.REGULAR((4,)), dma((6,)), dma((6,)), dma((3, 4)), dma((3, 4)), dma((2,)), dma((2,)),
        dma((2, 6)), dma((2, 6)),
    ]
    spec = pl.BlockSpec(memory_space=pl.ANY)
    shapes = (
        jax.ShapeDtypeStruct((512, 512), BF),
        jax.ShapeDtypeStruct((512, 1024), BF),
        jax.ShapeDtypeStruct((512, 512), BF),
    )
    outs = pl.pallas_call(
        kernel,
        out_shape=shapes,
        in_specs=[pl.BlockSpec(memory_space=pltpu.HBM)] * 6,
        out_specs=(spec,) * 3,
        scratch_shapes=scratch,
        compiler_params=pltpu.CompilerParams(
            collective_id=0, has_side_effects=True, vmem_limit_bytes=58 * 1024 * 1024
        ),
        cost_estimate=pl.CostEstimate(flops=8 * 10**9, bytes_accessed=10**7, transcendentals=0),
    )(inputs, rows_b, rows_c, log_decay, score_cotangent, out_weight)
    return pl.pallas_call(
        hand_on,
        out_shape=shapes,
        in_specs=[pl.BlockSpec(memory_space=vm)] * 3,
        out_specs=(spec,) * 3,
        scratch_shapes=[dma((3,))],
        cost_estimate=pl.CostEstimate(flops=0, bytes_accessed=4 * 2**20, transcendentals=0),
    )(*outs)


def solution(mesh):
    return jax.shard_map(
        local,
        mesh=mesh,
        in_specs=(
            P("seq", "head"),
            P("seq", None),
            P("seq", None),
            P("head", "seq"),
            P("seq", "head"),
            P("head", None),
        ),
        out_specs=(P("seq", "head"), P("seq", "head"), P("seq", "head")),
        check_vma=False,
    )
```

```python
import functools

import jax
import jax.numpy as jnp
from jax import lax
from jax.experimental import pallas as pl
from jax.experimental.pallas import tpu as pltpu
from jax.sharding import PartitionSpec as P

Q = 256
F32 = jnp.float32
BF = jnp.bfloat16
MESH = pl.DeviceIdType.MESH
CHIPS = 32
LO, HI = slice(0, Q), slice(Q, 2 * Q)


def mm(a, b):
    return jnp.dot(a, b, preferred_element_type=F32)


def mm_nt(a, b):
    return lax.dot_general(a, b, (((1,), (1,)), ((), ())), preferred_element_type=F32)


def kernel(
    x_hbm, b_hbm, c_hbm, ld_hbm, sc_hbm, w_hbm,
    ch_hbm, ig_hbm, sg_hbm,
    x_ref, b_ref, c_ref, ld_ref, sc_ref, ch_ref, ig_ref, sg_ref, w_v, rise_x, tw_x, bT, cT, cum, g_row, cumT, gT, sco, scoT, mix, mixT, dec,
    yl, vl, mid, end, sin, pulled, mixed, gbuf,
    ep_src, ep_dst, tot, rbuf, pbuf, sbuf, sp_src, sp_dst, dt, dtp, dchip, dall,
    pblk, ropp, from_l, from_r,
    in_sem, out_sem, round_sem, ag_s, ag_r, ex_s, ex_r, d_s, d_r, rs_s, rs_r,
):
    s_idx, hx = lax.axis_index("seq"), lax.axis_index("head")
    chip, core = s_idx // 2, lax.rem(s_idx, 2)
    right, left, opp = lax.rem(hx + 1, 4), lax.rem(hx + 3, 4), lax.rem(hx + 2, 4)
    dev_r, dev_l = (s_idx, right), (s_idx, left)
    dev_p = (2 * chip + 1 - core, hx)

    def rcopy(src, dst, ssem, rsem, dev):
        return pltpu.make_async_remote_copy(
            src_ref=src, dst_ref=dst, send_sem=ssem, recv_sem=rsem,
            device_id=dev, device_id_type=MESH,
        )

    y, z = chip // 8, lax.rem(chip, 8)

    def along_z(o):
        return (2 * (8 * y + lax.rem(z + o, 8)) + core, hx)

    def along_y(o):
        return (2 * (8 * lax.rem(y + o, 4) + z) + core, hx)

    barrier = pltpu.get_barrier_semaphore()
    for dev in (dev_r, dev_l, dev_p, along_z(1), along_z(7), along_y(1), along_y(3)):
        pl.semaphore_signal(barrier, inc=1, device_id=dev, device_id_type=MESH)
    loads = [
        pltpu.make_async_copy(src, dst, in_sem.at[i])
        for i, (src, dst) in enumerate(
            (
                (sc_hbm, sc_ref), (ld_hbm, ld_ref), (b_hbm, b_ref),
                (c_hbm, c_ref), (x_hbm, x_ref), (w_hbm, w_v),
            )
        )
    ]
    for copy in loads[:5]:
        copy.start()
    loads[0].wait()
    pl.semaphore_wait(barrier, 7)

    def tell(i, devs):
        for dev in devs:
            pl.semaphore_signal(round_sem.at[i], inc=1, device_id=dev, device_id_type=MESH)

    def heard(i):
        pl.semaphore_wait(round_sem.at[i], 2)

    ag = [
        rcopy(sc_ref.at[LO], gbuf.at[hx, LO], ag_s.at[0], ag_r.at[0], dev_r),
        rcopy(sc_ref.at[HI], gbuf.at[hx, HI], ag_s.at[1], ag_r.at[1], dev_l),
        rcopy(sc_ref.at[HI], gbuf.at[hx, HI], ag_s.at[2], ag_r.at[2], dev_r),
        rcopy(sc_ref.at[LO], gbuf.at[hx, LO], ag_s.at[3], ag_r.at[3], dev_l),
        rcopy(gbuf.at[left, LO], gbuf.at[left, LO], ag_s.at[4], ag_r.at[4], dev_r),
        rcopy(gbuf.at[right, HI], gbuf.at[right, HI], ag_s.at[5], ag_r.at[5], dev_l),
    ]
    for copy in ag[:4]:
        copy.start()
    loads[5].start()
    tell(0, (along_z(1), along_z(7)))
    for copy in loads[1:4]:
        copy.wait()

    spread = (
        lax.broadcasted_iota(jnp.int32, (16, 1024), 0)
        == lax.shift_right_logical(lax.broadcasted_iota(jnp.int32, (16, 1024), 1), 6)
    ).astype(F32)
    spread_b = spread.astype(BF)
    lane = lax.broadcasted_iota(jnp.int32, (16, Q), 1)
    for blk in range(2):
        at = slice(blk * Q, (blk + 1) * Q)
        ld = ld_ref[:, at]
        u = -2.0 * ld
        series = jnp.ones_like(u)
        for k in range(9, 1, -1):
            series = 1.0 - u * (1.0 / k) * series
        log_w = 0.5 * jnp.log(jnp.where(u < 0.5, u * series, 1.0 - jnp.exp(-u)))
        c = ld
        for k in (1, 2, 4, 8, 16, 32, 64, 128):
            c = c + jnp.where(lane >= k, pltpu.roll(c, k, 1), 0.0)
        total = c[:, Q - 1 : Q]
        g = c - log_w
        cum[:, at] = c
        g_row[:, at] = g
        cumT[at, :] = c.T
        gT[at, :] = g.T
        rise_x[at, :] = mm(jnp.exp(c).T.astype(BF), spread_b).astype(BF)
        tw_x[at, :] = mm(jnp.exp(total - g).T.astype(BF), spread_b).astype(BF)
        dec[blk : blk + 1, :] = jnp.sum(spread * jnp.exp(total), axis=0, keepdims=True)
    heard(0)
    tell(1, (along_z(2), along_z(6)))
    d_dev = dec[0:1, :] * dec[1:2, :]
    dec[2:3, :] = d_dev
    for r in range(8):
        dt[r : r + 1, :] = d_dev[:, 128 * r : 128 * r + 128]
    bT[...] = b_ref[...].astype(F32).T.astype(BF)
    cT[...] = c_ref[...].astype(F32).T.astype(BF)
    low = lax.broadcasted_iota(jnp.int32, (Q, Q), 0) >= lax.broadcasted_iota(jnp.int32, (Q, Q), 1)
    high = lax.broadcasted_iota(jnp.int32, (Q, Q), 0) <= lax.broadcasted_iota(jnp.int32, (Q, Q), 1)
    for blk in range(2):
        at = slice(blk * Q, (blk + 1) * Q)
        sco[blk] = jnp.where(low, mm(c_ref[at, :], bT[:, at]), 0.0)
        scoT[blk] = jnp.where(high, mm(b_ref[at, :], cT[:, at]), 0.0)

    def make_table(table, rows_f, cols_f, score):
        def body(g, carry):
            for i in range(2):
                h = 2 * g + i
                onehot = lax.broadcasted_iota(jnp.int32, (Q, 16), 1) == h
                for blk in range(2):
                    at = slice(blk * Q, (blk + 1) * Q)
                    col = jnp.sum(jnp.where(onehot, cols_f[at, :], 0.0), axis=1, keepdims=True)
                    row = rows_f[pl.ds(h, 1), at]
                    gap = col - row if table is mix else row - col
                    value = jnp.exp(jnp.minimum(gap, 0.0)) * score[blk]
                    table[g, blk, :, i * Q : (i + 1) * Q] = value.astype(BF)
            return carry

        lax.fori_loop(0, 8, body, 0)

    lane_a = (lax.broadcasted_iota(jnp.int32, (Q, 128), 1) < 64).astype(F32)
    mask_a, mask_b = lane_a.astype(BF), (1.0 - lane_a).astype(BF)

    def intra(src, table, out):
        def body(g, carry):
            cols = pl.ds(pl.multiple_of(g * 128, 128), 128)
            for blk in range(2):
                at = slice(blk * Q, (blk + 1) * Q)
                z = src[at, cols]
                both = jnp.concatenate([z * mask_a, z * mask_b], axis=0)
                out[at, cols] = mm(table[g, blk], both)
            return carry

        lax.fori_loop(0, 8, body, 0)

    def end_state(k, src, scale, mapT, fwd, base):
        def body(q, carry):
            cols = pl.ds(pl.multiple_of(base + q * 256, 256), 256)
            p0 = mm(mapT[:, LO], src[LO, cols] * scale[LO, cols])
            p1 = mm(mapT[:, HI], src[HI, cols] * scale[HI, cols])
            if fwd:
                mid[k, :, cols] = p0
                end[k, :, cols] = dec[1:2, cols] * p0 + p1
            else:
                mid[k, :, cols] = p1
                end[k, :, cols] = dec[0:1, cols] * p1 + p0
            return carry

        lax.fori_loop(0, 2, body, 0)

    def finish(k, rows, local, scale, out, fwd, base, factor=None):
        def body(q, carry):
            cols = pl.ds(pl.multiple_of(base + q * 256, 256), 256)
            s = sin[k, :, cols]
            if fwd:
                s0, s1 = s, mid[k, :, cols] + dec[0:1, cols] * s
            else:
                s1, s0 = s, mid[k, :, cols] + dec[1:2, cols] * s
            for at, state in ((LO, s0), (HI, s1)):
                value = local[at, cols] + scale[at, cols].astype(F32) * mm(
                    rows[at, :], state.astype(BF)
                )
                if factor is not None:
                    value = factor * value
                out[at, cols] = value.astype(BF)
            return carry

        lax.fori_loop(0, 2, body, 0)

    near, far = core * 512, (1 - core) * 512
    mine = pl.ds(pl.multiple_of(near, 512), 512)
    other = pl.ds(pl.multiple_of(far, 512), 512)
    core_f = core.astype(F32)
    decay_row = 4 * core + lax.rem(chip, 4)

    def far_first(o):
        j, k = o // 8, lax.rem(o, 8)
        dz = 4 + (k // 2) - lax.rem(k, 2) * (k // 2 + (k + 1) // 2)
        dy = 2 + (j // 2) - lax.rem(j, 2) * (j // 2 + (j + 1) // 2)
        return 8 * lax.rem(y + dy, 4) + lax.rem(z + dz, 8)

    def spread_out(src, dst, ssem, rsem):
        def body(o, carry):
            d = far_first(o)
            rcopy(src.at[d], dst.at[chip], ssem, rsem, (2 * d + core, hx)).start()
            return carry

        lax.fori_loop(0, CHIPS - 1, body, 0)

    def all_of(src, dst, ssem, rsem):
        part = pl.ds(0, CHIPS - 1)
        return rcopy(src.at[part], dst.at[part], ssem, rsem, dev_p)

    waits = []

    def ex_pair(k):
        ep_src[k] = end[k, :, other].astype(BF)
        rcopy(ep_src.at[k], ep_dst.at[k], ex_s.at[k, 0], ex_r.at[k, 0], dev_p).start()
        if k == 0:
            rcopy(dt, dtp, d_s.at[0], d_r.at[0], dev_p).start()

    def ex_out(k, fwd):
        copy = rcopy(ep_src.at[k], ep_dst.at[k], ex_s.at[k, 0], ex_r.at[k, 0], dev_p)
        copy.wait_recv()
        waits.append(copy)
        if k == 0:
            copy = rcopy(dt, dtp, d_s.at[0], d_r.at[0], dev_p)
            copy.wait_recv()
            waits.append(copy)
            dchip[...] = dt[...] * dtp[...]
            for r in range(8):
                dec[3:4, 128 * r : 128 * r + 128] = dtp[r : r + 1, :]
            dall[pl.ds(chip, 1)] = dchip[...][None]

            def body(o, carry):
                d = far_first(o)
                rcopy(dchip, dall.at[chip], d_s.at[1], d_r.at[1], (2 * d + core, hx)).start()
                return carry

            lax.fori_loop(0, CHIPS - 1, body, 0)
        first = 1.0 - core_f if fwd else core_f
        d_me, d_p = dec[2:3, mine], dec[3:4, mine]
        value = (1.0 - first + first * d_p) * end[k, :, mine] + (
            first + (1.0 - first) * d_me
        ) * ep_dst[k].astype(F32)
        value = value.astype(BF)
        for i in range(8):
            for j in range(4):
                tot[k, 4 * i + j] = value[16 * i : 16 * i + 16, 128 * j : 128 * j + 128]
        rbuf[k, pl.ds(chip, 1)] = tot[k, pl.ds(chip, 1)]
        spread_out(tot.at[k], rbuf.at[k], ex_s.at[k, 1], ex_r.at[k, 1])

    def ex_back(k, fwd):
        copy = all_of(tot.at[k], rbuf.at[k], ex_s.at[k, 1], ex_r.at[k, 1])
        copy.wait_recv()
        waits.append(copy)
        if k == 0:
            part = pl.ds(0, CHIPS - 1)
            copy = rcopy(dall.at[part], dall.at[part], d_s.at[1], d_r.at[1], dev_p)
            copy.wait_recv()
            waits.append(copy)
        run = jnp.zeros((16, 128), F32)
        for e in range(CHIPS) if fwd else range(CHIPS - 1, -1, -1):
            pbuf[k, e] = run.astype(BF)
            run = run * dall[e, pl.ds(decay_row, 1), :] + rbuf[k, e].astype(F32)
        sbuf[k, pl.ds(chip, 1)] = pbuf[k, pl.ds(chip, 1)]
        spread_out(pbuf.at[k], sbuf.at[k], ex_s.at[k, 2], ex_r.at[k, 2])

    def ex_split(k, fwd):
        copy = all_of(pbuf.at[k], sbuf.at[k], ex_s.at[k, 2], ex_r.at[k, 2])
        copy.wait_recv()
        waits.append(copy)
        first = 1.0 - core_f if fwd else core_f
        for j in range(4):
            cols = pl.ds(pl.multiple_of(core * 512 + 128 * j, 128), 128)
            d_me, d_p = dec[2:3, cols], dec[3:4, cols]
            for i in range(8):
                at = slice(16 * i, 16 * i + 16)
                s = sbuf[k, 4 * i + j].astype(F32)
                theirs = (1.0 - first + first * d_me) * s + first * end[k, at, cols]
                sp_src[k, at, 128 * j : 128 * j + 128] = theirs.astype(BF)
                e_p = ep_dst[k, at, 128 * j : 128 * j + 128].astype(F32)
                sin[k, at, cols] = (first + (1.0 - first) * d_p) * s + (1.0 - first) * e_p
        rcopy(sp_src.at[k], sp_dst.at[k], ex_s.at[k, 3], ex_r.at[k, 3], dev_p).start()

    def ex_end(k):
        copy = rcopy(sp_src.at[k], sp_dst.at[k], ex_s.at[k, 3], ex_r.at[k, 3], dev_p)
        copy.wait_recv()
        waits.append(copy)
        sin[k, :, other] = sp_dst[k].astype(F32)

    def project(r, slot, dest, at):
        cols = pl.ds(pl.multiple_of(dest * 512, 512), 512)
        pblk[r, slot, at, :] = mm(mixed[at, :], w_v[:, cols]).astype(BF)

    def rs_copies(r):
        return [
            rcopy(pblk.at[r, 0, LO], ropp.at[r, 0], rs_s.at[r, 0], rs_r.at[r, 0], dev_r),
            rcopy(pblk.at[r, 0, HI], ropp.at[r, 1], rs_s.at[r, 1], rs_r.at[r, 1], dev_l),
            rcopy(pblk.at[r, 1, HI], from_l.at[r, HI], rs_s.at[r, 2], rs_r.at[r, 2], dev_r),
            rcopy(pblk.at[r, 2, LO], from_r.at[r, LO], rs_s.at[r, 3], rs_r.at[r, 3], dev_l),
            rcopy(pblk.at[r, 1, LO], from_l.at[r, LO], rs_s.at[r, 4], rs_r.at[r, 4], dev_r),
            rcopy(pblk.at[r, 2, HI], from_r.at[r, HI], rs_s.at[r, 5], rs_r.at[r, 5], dev_l),
        ]

    rs = [rs_copies(0), rs_copies(1)]

    def rs_first(r):
        project(r, 0, opp, LO)
        rs[r][0].start()
        project(r, 0, opp, HI)
        rs[r][1].start()

    def rs_second(r):
        project(r, 1, right, HI)
        rs[r][2].start()
        project(r, 2, left, LO)
        rs[r][3].start()
        project(r, 1, right, LO)
        project(r, 2, left, HI)
        project(r, 3, hx, LO)
        project(r, 3, hx, HI)

    def rs_mid(r):
        rs[r][0].wait_recv()
        pblk[r, 1, LO, :] = (pblk[r, 1, LO, :].astype(F32) + ropp[r, 0].astype(F32)).astype(BF)
        rs[r][4].start()
        rs[r][1].wait_recv()
        pblk[r, 2, HI, :] = (pblk[r, 2, HI, :].astype(F32) + ropp[r, 1].astype(F32)).astype(BF)
        rs[r][5].start()

    def rs_end(r, out):
        for copy in rs[r][2:]:
            copy.wait_recv()
        out[...] = (
            pblk[r, 3].astype(F32) + from_l[r].astype(F32) + from_r[r].astype(F32)
        ).astype(BF)

    def pull_first():
        def body(n, carry):
            rows = pl.ds(pl.multiple_of(n * Q, Q), Q)
            total = jnp.zeros((2 * Q, Q), F32)
            for block, dest in ((sc_ref, hx), (gbuf.at[left], left), (gbuf.at[right], right)):
                cols = pl.ds(pl.multiple_of(dest * 512, 512), 512)
                total = total + mm_nt(block[...], w_v[rows, cols])
            vl[:, rows] = total
            return carry

        lax.fori_loop(0, 4, body, 0)

    def pull_last(base):
        cols = pl.ds(pl.multiple_of(opp * 512, 512), 512)

        def body(n, carry):
            rows = pl.ds(pl.multiple_of(base + n * Q, Q), Q)
            pulled[:, rows] = (vl[:, rows] + mm_nt(gbuf[opp], w_v[rows, cols])).astype(BF)
            return carry

        lax.fori_loop(0, 2, body, 0)

    stores = [
        pltpu.make_async_copy(src, dst, out_sem.at[i])
        for i, (src, dst) in enumerate(((ch_ref, ch_hbm), (ig_ref, ig_hbm), (sg_ref, sg_hbm)))
    ]
    loads[4].wait()
    end_state(0, x_ref, tw_x, bT, True, far)
    end_state(0, x_ref, tw_x, bT, True, near)
    ex_pair(0)
    heard(1)
    tell(2, (along_y(1), along_y(3)))
    make_table(mix, g_row, cumT, sco)
    heard(2)
    tell(3, (along_y(1), along_y(3)))
    make_table(mixT, cum, gT, scoT)
    heard(3)
    ex_out(0, True)
    ag[0].wait_recv()
    ag[4].start()
    ag[1].wait_recv()
    ag[5].start()
    ag[2].wait_recv()
    ag[3].wait_recv()
    loads[5].wait()
    pull_first()
    ex_back(0, True)
    ag[4].wait_recv()
    ag[5].wait_recv()
    pull_last(far)
    end_state(1, pulled, rise_x, cT, False, far)
    ex_pair(1)
    pull_last(near)
    end_state(1, pulled, rise_x, cT, False, near)
    ex_out(1, False)
    intra(x_ref, mix, yl)
    ex_split(0, True)
    finish(0, c_ref, yl, rise_x, mixed, True, near)
    ex_end(0)
    finish(0, c_ref, yl, rise_x, mixed, True, far)
    rs_first(0)
    ex_back(1, False)
    rs_second(0)
    intra(pulled, mixT, vl)
    ex_split(1, False)
    finish(1, b_ref, vl, tw_x, ig_ref, False, near)
    end_state(2, ig_ref, tw_x, bT, True, near)
    ex_end(1)
    finish(1, b_ref, vl, tw_x, ig_ref, False, far)
    end_state(2, ig_ref, tw_x, bT, True, far)
    ex_pair(2)
    rs_mid(0)
    ex_out(2, True)
    stores[1].start()
    intra(ig_ref, mix, yl)
    ex_back(2, True)
    rs_end(0, ch_ref)
    stores[0].start()
    ex_split(2, True)
    finish(2, c_ref, yl, rise_x, mixed, True, near, 2.0)
    ex_end(2)
    finish(2, c_ref, yl, rise_x, mixed, True, far, 2.0)
    rs_first(1)
    rs_second(1)
    rs_mid(1)
    rs_end(1, sg_ref)
    stores[2].start()
    for copy in waits + ag + rs[0] + rs[1]:
        copy.wait_send()
    for copy in stores:
        copy.wait()


def hand_on(*refs):
    sources, results, held, in_sem, out_sem = refs[:3], refs[3:6], refs[6:9], refs[9], refs[10]
    order = (1, 0, 2)
    loads = [pltpu.make_async_copy(sources[i], held[i], in_sem.at[i]) for i in order]
    stores = [pltpu.make_async_copy(held[i], results[i], out_sem.at[i]) for i in order]
    for copy in loads:
        copy.start()
    for load, store in zip(loads, stores):
        load.wait()
        store.start()
    for copy in stores:
        copy.wait()


def local(inputs, rows_b, rows_c, log_decay, score_cotangent, out_weight):
    vm = pltpu.VMEM
    dma = pltpu.SemaphoreType.DMA
    scratch = [
        vm((512, 1024), BF), vm((512, 128), BF), vm((512, 128), BF), vm((16, 512), F32),
        vm((512, 512), BF), vm((512, 512), BF), vm((512, 1024), BF), vm((512, 512), BF),
        vm((1024, 2048), BF), vm((512, 1024), BF), vm((512, 1024), BF),
        vm((128, 512), BF), vm((128, 512), BF),
        vm((16, 512), F32), vm((16, 512), F32), vm((512, 16), F32), vm((512, 16), F32),
        vm((2, Q, Q), F32), vm((2, Q, Q), F32),
        vm((8, 2, Q, 2 * Q), BF), vm((8, 2, Q, 2 * Q), BF), vm((8, 1024), F32),
        vm((512, 1024), F32), vm((512, 1024), F32),
        vm((3, 128, 1024), F32), vm((3, 128, 1024), F32), vm((3, 128, 1024), F32),
        vm((512, 1024), BF), vm((512, 1024), BF), vm((4, 512, 512), BF),
        vm((3, 128, 512), BF), vm((3, 128, 512), BF),
        vm((3, CHIPS, 16, 128), BF), vm((3, CHIPS, 16, 128), BF),
        vm((3, CHIPS, 16, 128), BF), vm((3, CHIPS, 16, 128), BF),
        vm((3, 128, 512), BF), vm((3, 128, 512), BF),
        vm((8, 128), F32), vm((8, 128), F32), vm((8, 128), F32), vm((CHIPS, 8, 128), F32),
        vm((2, 4, 512, 512), BF), vm((2, 2, Q, 512), BF),
        vm((2, 512, 512), BF), vm((2, 512, 512), BF),
        dma((6,)), dma((3,)), pltpu.SemaphoreType.REGULAR((4,)), dma((6,)), dma((6,)), dma((3, 4)), dma((3, 4)), dma((2,)), dma((2,)),
        dma((2, 6)), dma((2, 6)),
    ]
    spec = pl.BlockSpec(memory_space=pl.ANY)
    shapes = (
        jax.ShapeDtypeStruct((512, 512), BF),
        jax.ShapeDtypeStruct((512, 1024), BF),
        jax.ShapeDtypeStruct((512, 512), BF),
    )
    outs = pl.pallas_call(
        kernel,
        out_shape=shapes,
        in_specs=[pl.BlockSpec(memory_space=pltpu.HBM)] * 6,
        out_specs=(spec,) * 3,
        scratch_shapes=scratch,
        compiler_params=pltpu.CompilerParams(
            collective_id=0, has_side_effects=True, vmem_limit_bytes=58 * 1024 * 1024
        ),
        cost_estimate=pl.CostEstimate(flops=8 * 10**9, bytes_accessed=10**7, transcendentals=0),
    )(inputs, rows_b, rows_c, log_decay, score_cotangent, out_weight)
    return pl.pallas_call(
        hand_on,
        out_shape=shapes,
        in_specs=[pl.BlockSpec(memory_space=pltpu.HBM)] * 3,
        out_specs=(spec,) * 3,
        scratch_shapes=[vm((512, 512), BF), vm((512, 1024), BF), vm((512, 512), BF)]
        + [dma((3,)), dma((3,))],
        cost_estimate=pl.CostEstimate(flops=0, bytes_accessed=4 * 2**20, transcendentals=0),
    )(*outs)


def solution(mesh):
    return jax.shard_map(
        local,
        mesh=mesh,
        in_specs=(
            P("seq", "head"),
            P("seq", None),
            P("seq", None),
            P("head", "seq"),
            P("seq", "head"),
            P("head", None),
        ),
        out_specs=(P("seq", "head"), P("seq", "head"), P("seq", "head")),
        check_vma=False,
    )
```

```python
import functools

import jax
import jax.numpy as jnp
from jax import lax
from jax.experimental import pallas as pl
from jax.experimental.pallas import tpu as pltpu
from jax.sharding import PartitionSpec as P

Q = 256
F32 = jnp.float32
BF = jnp.bfloat16
MESH = pl.DeviceIdType.MESH
CHIPS = 32
LO, HI = slice(0, Q), slice(Q, 2 * Q)


def mm(a, b):
    return jnp.dot(a, b, preferred_element_type=F32)


def mm_nt(a, b):
    return lax.dot_general(a, b, (((1,), (1,)), ((), ())), preferred_element_type=F32)


def kernel(
    x_hbm, b_hbm, c_hbm, ld_hbm, sc_hbm, w_hbm,
    ch_hbm, ig_hbm, own_hbm, left_hbm, right_hbm,
    x_ref, b_ref, c_ref, ld_ref, sc_ref, ch_ref, ig_ref, w_v, rise_x, tw_x, bT, cT, cum, g_row, cumT, gT, sco, scoT, mix, mixT, dec,
    yl, vl, mid, end, sin, pulled, mixed, gbuf,
    ep_src, ep_dst, tot, rbuf, pbuf, sbuf, sp_src, sp_dst, dt, dtp, dchip, dall,
    pblk, ropp, from_l, from_r,
    in_sem, out_sem, round_sem, ag_s, ag_r, ex_s, ex_r, d_s, d_r, rs_s, rs_r,
):
    s_idx, hx = lax.axis_index("seq"), lax.axis_index("head")
    chip, core = s_idx // 2, lax.rem(s_idx, 2)
    right, left, opp = lax.rem(hx + 1, 4), lax.rem(hx + 3, 4), lax.rem(hx + 2, 4)
    dev_r, dev_l = (s_idx, right), (s_idx, left)
    dev_p = (2 * chip + 1 - core, hx)

    def rcopy(src, dst, ssem, rsem, dev):
        return pltpu.make_async_remote_copy(
            src_ref=src, dst_ref=dst, send_sem=ssem, recv_sem=rsem,
            device_id=dev, device_id_type=MESH,
        )

    y, z = chip // 8, lax.rem(chip, 8)

    def along_z(o):
        return (2 * (8 * y + lax.rem(z + o, 8)) + core, hx)

    def along_y(o):
        return (2 * (8 * lax.rem(y + o, 4) + z) + core, hx)

    barrier = pltpu.get_barrier_semaphore()
    for dev in (dev_r, dev_l, dev_p, along_z(1), along_z(7), along_y(1), along_y(3)):
        pl.semaphore_signal(barrier, inc=1, device_id=dev, device_id_type=MESH)
    loads = [
        pltpu.make_async_copy(src, dst, in_sem.at[i])
        for i, (src, dst) in enumerate(
            (
                (sc_hbm, sc_ref), (ld_hbm, ld_ref), (b_hbm, b_ref),
                (c_hbm, c_ref), (x_hbm, x_ref), (w_hbm, w_v),
            )
        )
    ]
    for copy in loads[:5]:
        copy.start()
    pl.semaphore_wait(barrier, 7)

    def tell(i, devs):
        for dev in devs:
            pl.semaphore_signal(round_sem.at[i], inc=1, device_id=dev, device_id_type=MESH)

    def heard(i):
        pl.semaphore_wait(round_sem.at[i], 2)

    ag = [
        rcopy(sc_hbm.at[LO], gbuf.at[hx, LO], ag_s.at[0], ag_r.at[0], dev_r),
        rcopy(sc_hbm.at[HI], gbuf.at[hx, HI], ag_s.at[1], ag_r.at[1], dev_l),
        rcopy(sc_hbm.at[HI], gbuf.at[hx, HI], ag_s.at[2], ag_r.at[2], dev_r),
        rcopy(sc_hbm.at[LO], gbuf.at[hx, LO], ag_s.at[3], ag_r.at[3], dev_l),
        rcopy(gbuf.at[left, LO], gbuf.at[left, LO], ag_s.at[4], ag_r.at[4], dev_r),
        rcopy(gbuf.at[right, HI], gbuf.at[right, HI], ag_s.at[5], ag_r.at[5], dev_l),
    ]
    for copy in ag[:4]:
        copy.start()
    loads[5].start()
    tell(0, (along_z(1), along_z(7)))
    for copy in loads[1:4]:
        copy.wait()

    spread = (
        lax.broadcasted_iota(jnp.int32, (16, 1024), 0)
        == lax.shift_right_logical(lax.broadcasted_iota(jnp.int32, (16, 1024), 1), 6)
    ).astype(F32)
    spread_b = spread.astype(BF)
    lane = lax.broadcasted_iota(jnp.int32, (16, Q), 1)
    for blk in range(2):
        at = slice(blk * Q, (blk + 1) * Q)
        ld = ld_ref[:, at]
        u = -2.0 * ld
        series = jnp.ones_like(u)
        for k in range(9, 1, -1):
            series = 1.0 - u * (1.0 / k) * series
        log_w = 0.5 * jnp.log(jnp.where(u < 0.5, u * series, 1.0 - jnp.exp(-u)))
        c = ld
        for k in (1, 2, 4, 8, 16, 32, 64, 128):
            c = c + jnp.where(lane >= k, pltpu.roll(c, k, 1), 0.0)
        total = c[:, Q - 1 : Q]
        g = c - log_w
        cum[:, at] = c
        g_row[:, at] = g
        cumT[at, :] = c.T
        gT[at, :] = g.T
        rise_x[at, :] = mm(jnp.exp(c).T.astype(BF), spread_b).astype(BF)
        tw_x[at, :] = mm(jnp.exp(total - g).T.astype(BF), spread_b).astype(BF)
        dec[blk : blk + 1, :] = jnp.sum(spread * jnp.exp(total), axis=0, keepdims=True)
    heard(0)
    tell(1, (along_z(2), along_z(6)))
    d_dev = dec[0:1, :] * dec[1:2, :]
    dec[2:3, :] = d_dev
    for r in range(8):
        dt[r : r + 1, :] = d_dev[:, 128 * r : 128 * r + 128]
    bT[...] = b_ref[...].astype(F32).T.astype(BF)
    cT[...] = c_ref[...].astype(F32).T.astype(BF)
    low = lax.broadcasted_iota(jnp.int32, (Q, Q), 0) >= lax.broadcasted_iota(jnp.int32, (Q, Q), 1)
    high = lax.broadcasted_iota(jnp.int32, (Q, Q), 0) <= lax.broadcasted_iota(jnp.int32, (Q, Q), 1)
    for blk in range(2):
        at = slice(blk * Q, (blk + 1) * Q)
        sco[blk] = jnp.where(low, mm(c_ref[at, :], bT[:, at]), 0.0)
        scoT[blk] = jnp.where(high, mm(b_ref[at, :], cT[:, at]), 0.0)

    def make_table(table, rows_f, cols_f, score):
        def body(g, carry):
            for i in range(2):
                h = 2 * g + i
                onehot = lax.broadcasted_iota(jnp.int32, (Q, 16), 1) == h
                for blk in range(2):
                    at = slice(blk * Q, (blk + 1) * Q)
                    col = jnp.sum(jnp.where(onehot, cols_f[at, :], 0.0), axis=1, keepdims=True)
                    row = rows_f[pl.ds(h, 1), at]
                    gap = col - row if table is mix else row - col
                    value = jnp.exp(jnp.minimum(gap, 0.0)) * score[blk]
                    table[g, blk, :, i * Q : (i + 1) * Q] = value.astype(BF)
            return carry

        lax.fori_loop(0, 8, body, 0)

    lane_a = (lax.broadcasted_iota(jnp.int32, (Q, 128), 1) < 64).astype(F32)
    mask_a, mask_b = lane_a.astype(BF), (1.0 - lane_a).astype(BF)

    def intra(src, table, out):
        def body(g, carry):
            cols = pl.ds(pl.multiple_of(g * 128, 128), 128)
            for blk in range(2):
                at = slice(blk * Q, (blk + 1) * Q)
                z = src[at, cols]
                both = jnp.concatenate([z * mask_a, z * mask_b], axis=0)
                out[at, cols] = mm(table[g, blk], both)
            return carry

        lax.fori_loop(0, 8, body, 0)

    def end_state(k, src, scale, mapT, fwd, base):
        def body(q, carry):
            cols = pl.ds(pl.multiple_of(base + q * 256, 256), 256)
            p0 = mm(mapT[:, LO], src[LO, cols] * scale[LO, cols])
            p1 = mm(mapT[:, HI], src[HI, cols] * scale[HI, cols])
            if fwd:
                mid[k, :, cols] = p0
                end[k, :, cols] = dec[1:2, cols] * p0 + p1
            else:
                mid[k, :, cols] = p1
                end[k, :, cols] = dec[0:1, cols] * p1 + p0
            return carry

        lax.fori_loop(0, 2, body, 0)

    def finish(k, rows, local, scale, out, fwd, base, factor=None):
        def body(q, carry):
            cols = pl.ds(pl.multiple_of(base + q * 256, 256), 256)
            s = sin[k, :, cols]
            if fwd:
                s0, s1 = s, mid[k, :, cols] + dec[0:1, cols] * s
            else:
                s1, s0 = s, mid[k, :, cols] + dec[1:2, cols] * s
            for at, state in ((LO, s0), (HI, s1)):
                value = local[at, cols] + scale[at, cols].astype(F32) * mm(
                    rows[at, :], state.astype(BF)
                )
                if factor is not None:
                    value = factor * value
                out[at, cols] = value.astype(BF)
            return carry

        lax.fori_loop(0, 2, body, 0)

    near, far = core * 512, (1 - core) * 512
    mine = pl.ds(pl.multiple_of(near, 512), 512)
    other = pl.ds(pl.multiple_of(far, 512), 512)
    core_f = core.astype(F32)
    decay_row = 4 * core + lax.rem(chip, 4)

    at_y = [lax.rem(y + dy, 4) for dy in range(4)]
    at_z = [lax.rem(z + dz, 8) for dz in range(8)]
    others = [
        8 * at_y[dy] + at_z[dz]
        for dy in (2, 1, 3, 0)
        for dz in (4, 3, 5, 2, 6, 1, 7, 0)
        if (dy, dz) != (0, 0)
    ]

    def spread_out(src, dst, ssem, rsem):
        for d in others:
            rcopy(src.at[d], dst.at[chip], ssem, rsem, (2 * d + core, hx)).start()

    def all_of(src, dst, ssem, rsem):
        part = pl.ds(0, CHIPS - 1)
        return rcopy(src.at[part], dst.at[part], ssem, rsem, dev_p)

    waits = []

    def ex_pair(k):
        ep_src[k] = end[k, :, other].astype(BF)
        rcopy(ep_src.at[k], ep_dst.at[k], ex_s.at[k, 0], ex_r.at[k, 0], dev_p).start()
        if k == 0:
            rcopy(dt, dtp, d_s.at[0], d_r.at[0], dev_p).start()

    def ex_out(k, fwd):
        copy = rcopy(ep_src.at[k], ep_dst.at[k], ex_s.at[k, 0], ex_r.at[k, 0], dev_p)
        copy.wait_recv()
        waits.append(copy)
        if k == 0:
            copy = rcopy(dt, dtp, d_s.at[0], d_r.at[0], dev_p)
            copy.wait_recv()
            waits.append(copy)
            dchip[...] = dt[...] * dtp[...]
            for r in range(8):
                dec[3:4, 128 * r : 128 * r + 128] = dtp[r : r + 1, :]
            dall[pl.ds(chip, 1)] = dchip[...][None]

            for d in others:
                rcopy(dchip, dall.at[chip], d_s.at[1], d_r.at[1], (2 * d + core, hx)).start()
        first = 1.0 - core_f if fwd else core_f
        d_me, d_p = dec[2:3, mine], dec[3:4, mine]
        value = (1.0 - first + first * d_p) * end[k, :, mine] + (
            first + (1.0 - first) * d_me
        ) * ep_dst[k].astype(F32)
        value = value.astype(BF)
        for i in range(8):
            for j in range(4):
                tot[k, 4 * i + j] = value[16 * i : 16 * i + 16, 128 * j : 128 * j + 128]
        rbuf[k, pl.ds(chip, 1)] = tot[k, pl.ds(chip, 1)]
        spread_out(tot.at[k], rbuf.at[k], ex_s.at[k, 1], ex_r.at[k, 1])

    def ex_back(k, fwd):
        copy = all_of(tot.at[k], rbuf.at[k], ex_s.at[k, 1], ex_r.at[k, 1])
        copy.wait_recv()
        waits.append(copy)
        if k == 0:
            part = pl.ds(0, CHIPS - 1)
            copy = rcopy(dall.at[part], dall.at[part], d_s.at[1], d_r.at[1], dev_p)
            copy.wait_recv()
            waits.append(copy)
        run = jnp.zeros((16, 128), F32)
        for e in range(CHIPS) if fwd else range(CHIPS - 1, -1, -1):
            pbuf[k, e] = run.astype(BF)
            run = run * dall[e, pl.ds(decay_row, 1), :] + rbuf[k, e].astype(F32)
        sbuf[k, pl.ds(chip, 1)] = pbuf[k, pl.ds(chip, 1)]
        spread_out(pbuf.at[k], sbuf.at[k], ex_s.at[k, 2], ex_r.at[k, 2])

    def ex_split(k, fwd):
        copy = all_of(pbuf.at[k], sbuf.at[k], ex_s.at[k, 2], ex_r.at[k, 2])
        copy.wait_recv()
        waits.append(copy)
        first = 1.0 - core_f if fwd else core_f
        for j in range(4):
            cols = pl.ds(pl.multiple_of(core * 512 + 128 * j, 128), 128)
            d_me, d_p = dec[2:3, cols], dec[3:4, cols]
            for i in range(8):
                at = slice(16 * i, 16 * i + 16)
                s = sbuf[k, 4 * i + j].astype(F32)
                theirs = (1.0 - first + first * d_me) * s + first * end[k, at, cols]
                sp_src[k, at, 128 * j : 128 * j + 128] = theirs.astype(BF)
                e_p = ep_dst[k, at, 128 * j : 128 * j + 128].astype(F32)
                sin[k, at, cols] = (first + (1.0 - first) * d_p) * s + (1.0 - first) * e_p
        rcopy(sp_src.at[k], sp_dst.at[k], ex_s.at[k, 3], ex_r.at[k, 3], dev_p).start()

    def ex_end(k):
        copy = rcopy(sp_src.at[k], sp_dst.at[k], ex_s.at[k, 3], ex_r.at[k, 3], dev_p)
        copy.wait_recv()
        waits.append(copy)
        sin[k, :, other] = sp_dst[k].astype(F32)

    def project(r, slot, dest, at):
        cols = pl.ds(pl.multiple_of(dest * 512, 512), 512)
        pblk[r, slot, at, :] = mm(mixed[at, :], w_v[:, cols]).astype(BF)

    def rs_copies(r):
        into_l = left_hbm if r else from_l
        into_r = right_hbm if r else from_r
        return [
            rcopy(pblk.at[r, 0, LO], ropp.at[r, 0], rs_s.at[r, 0], rs_r.at[r, 0], dev_r),
            rcopy(pblk.at[r, 0, HI], ropp.at[r, 1], rs_s.at[r, 1], rs_r.at[r, 1], dev_l),
            rcopy(pblk.at[r, 1, HI], into_l.at[HI], rs_s.at[r, 2], rs_r.at[r, 2], dev_r),
            rcopy(pblk.at[r, 2, LO], into_r.at[LO], rs_s.at[r, 3], rs_r.at[r, 3], dev_l),
            rcopy(pblk.at[r, 1, LO], into_l.at[LO], rs_s.at[r, 4], rs_r.at[r, 4], dev_r),
            rcopy(pblk.at[r, 2, HI], into_r.at[HI], rs_s.at[r, 5], rs_r.at[r, 5], dev_l),
        ]

    rs = [rs_copies(0), rs_copies(1)]

    def rs_first(r):
        project(r, 0, opp, LO)
        rs[r][0].start()
        project(r, 0, opp, HI)
        rs[r][1].start()

    def rs_second(r):
        project(r, 1, right, HI)
        rs[r][2].start()
        project(r, 2, left, LO)
        rs[r][3].start()
        project(r, 1, right, LO)
        project(r, 2, left, HI)
        project(r, 3, hx, LO)
        project(r, 3, hx, HI)

    def rs_mid(r):
        rs[r][0].wait_recv()
        pblk[r, 1, LO, :] = (pblk[r, 1, LO, :].astype(F32) + ropp[r, 0].astype(F32)).astype(BF)
        rs[r][4].start()
        rs[r][1].wait_recv()
        pblk[r, 2, HI, :] = (pblk[r, 2, HI, :].astype(F32) + ropp[r, 1].astype(F32)).astype(BF)
        rs[r][5].start()

    def rs_end(r, out):
        for copy in rs[r][2:]:
            copy.wait_recv()
        if out is not None:
            out[...] = (
                pblk[r, 3].astype(F32) + from_l[...].astype(F32) + from_r[...].astype(F32)
            ).astype(BF)

    def pull_first():
        def body(n, carry):
            rows = pl.ds(pl.multiple_of(n * Q, Q), Q)
            total = jnp.zeros((2 * Q, Q), F32)
            for block, dest in ((sc_ref, hx), (gbuf.at[left], left), (gbuf.at[right], right)):
                cols = pl.ds(pl.multiple_of(dest * 512, 512), 512)
                total = total + mm_nt(block[...], w_v[rows, cols])
            vl[:, rows] = total
            return carry

        lax.fori_loop(0, 4, body, 0)

    def pull_last(base):
        cols = pl.ds(pl.multiple_of(opp * 512, 512), 512)

        def body(n, carry):
            rows = pl.ds(pl.multiple_of(base + n * Q, Q), Q)
            pulled[:, rows] = (vl[:, rows] + mm_nt(gbuf[opp], w_v[rows, cols])).astype(BF)
            return carry

        lax.fori_loop(0, 2, body, 0)

    stores = [
        pltpu.make_async_copy(src, dst, out_sem.at[i])
        for i, (src, dst) in enumerate(((ch_ref, ch_hbm), (ig_ref, ig_hbm), (pblk.at[1, 3], own_hbm)))
    ]
    loads[4].wait()
    end_state(0, x_ref, tw_x, bT, True, far)
    end_state(0, x_ref, tw_x, bT, True, near)
    ex_pair(0)
    heard(1)
    tell(2, (along_y(1), along_y(3)))
    make_table(mix, g_row, cumT, sco)
    heard(2)
    tell(3, (along_y(1), along_y(3)))
    make_table(mixT, cum, gT, scoT)
    ag[0].wait_recv()
    ag[4].start()
    ag[1].wait_recv()
    ag[5].start()
    heard(3)
    ex_out(0, True)
    ag[2].wait_recv()
    ag[3].wait_recv()
    loads[0].wait()
    loads[5].wait()
    pull_first()
    ex_back(0, True)
    ag[4].wait_recv()
    ag[5].wait_recv()
    pull_last(far)
    end_state(1, pulled, rise_x, cT, False, far)
    ex_pair(1)
    pull_last(near)
    end_state(1, pulled, rise_x, cT, False, near)
    ex_out(1, False)
    intra(x_ref, mix, yl)
    ex_split(0, True)
    finish(0, c_ref, yl, rise_x, mixed, True, near)
    ex_end(0)
    finish(0, c_ref, yl, rise_x, mixed, True, far)
    rs_first(0)
    ex_back(1, False)
    rs_second(0)
    intra(pulled, mixT, vl)
    ex_split(1, False)
    finish(1, b_ref, vl, tw_x, ig_ref, False, near)
    end_state(2, ig_ref, tw_x, bT, True, near)
    ex_end(1)
    finish(1, b_ref, vl, tw_x, ig_ref, False, far)
    end_state(2, ig_ref, tw_x, bT, True, far)
    ex_pair(2)
    rs_mid(0)
    ex_out(2, True)
    stores[1].start()
    intra(ig_ref, mix, yl)
    ex_back(2, True)
    rs_end(0, ch_ref)
    stores[0].start()
    ex_split(2, True)
    finish(2, c_ref, yl, rise_x, mixed, True, near, 2.0)
    ex_end(2)
    finish(2, c_ref, yl, rise_x, mixed, True, far, 2.0)
    rs_first(1)
    rs_second(1)
    stores[2].start()
    rs_mid(1)
    rs_end(1, None)
    for copy in waits + ag + rs[0] + rs[1]:
        copy.wait_send()
    for copy in stores:
        copy.wait()


def hand_on(*refs):
    sources, results, held, total, in_sem, out_sem = (
        refs[:5], refs[5:8], refs[8:13], refs[13], refs[14], refs[15]
    )
    loads = [pltpu.make_async_copy(sources[i], held[i], in_sem.at[i]) for i in range(5)]
    stores = [
        pltpu.make_async_copy(src, results[i], out_sem.at[i])
        for i, src in enumerate((held[0], held[1], total))
    ]
    for i in (2, 3, 4, 1, 0):
        loads[i].start()
    for i in (2, 3, 4):
        loads[i].wait()
    total[...] = (
        held[2][...].astype(F32) + held[3][...].astype(F32) + held[4][...].astype(F32)
    ).astype(BF)
    stores[2].start()
    for i in (1, 0):
        loads[i].wait()
        stores[i].start()
    for copy in stores:
        copy.wait()


def local(inputs, rows_b, rows_c, log_decay, score_cotangent, out_weight):
    vm = pltpu.VMEM
    dma = pltpu.SemaphoreType.DMA
    scratch = [
        vm((512, 1024), BF), vm((512, 128), BF), vm((512, 128), BF), vm((16, 512), F32),
        vm((512, 512), BF), vm((512, 512), BF), vm((512, 1024), BF),
        vm((1024, 2048), BF), vm((512, 1024), BF), vm((512, 1024), BF),
        vm((128, 512), BF), vm((128, 512), BF),
        vm((16, 512), F32), vm((16, 512), F32), vm((512, 16), F32), vm((512, 16), F32),
        vm((2, Q, Q), F32), vm((2, Q, Q), F32),
        vm((8, 2, Q, 2 * Q), BF), vm((8, 2, Q, 2 * Q), BF), vm((8, 1024), F32),
        vm((512, 1024), F32), vm((512, 1024), F32),
        vm((3, 128, 1024), F32), vm((3, 128, 1024), F32), vm((3, 128, 1024), F32),
        vm((512, 1024), BF), vm((512, 1024), BF), vm((4, 512, 512), BF),
        vm((3, 128, 512), BF), vm((3, 128, 512), BF),
        vm((3, CHIPS, 16, 128), BF), vm((3, CHIPS, 16, 128), BF),
        vm((3, CHIPS, 16, 128), BF), vm((3, CHIPS, 16, 128), BF),
        vm((3, 128, 512), BF), vm((3, 128, 512), BF),
        vm((8, 128), F32), vm((8, 128), F32), vm((8, 128), F32), vm((CHIPS, 8, 128), F32),
        vm((2, 4, 512, 512), BF), vm((2, 2, Q, 512), BF),
        vm((512, 512), BF), vm((512, 512), BF),
        dma((6,)), dma((3,)), pltpu.SemaphoreType.REGULAR((4,)), dma((6,)), dma((6,)), dma((3, 4)), dma((3, 4)), dma((2,)), dma((2,)),
        dma((2, 6)), dma((2, 6)),
    ]
    spec = pl.BlockSpec(memory_space=pl.ANY)
    shapes = (
        jax.ShapeDtypeStruct((512, 512), BF),
        jax.ShapeDtypeStruct((512, 1024), BF),
        jax.ShapeDtypeStruct((512, 512), BF),
    )
    outs = pl.pallas_call(
        kernel,
        out_shape=shapes + (shapes[0], shapes[0]),
        in_specs=[pl.BlockSpec(memory_space=pltpu.HBM)] * 6,
        out_specs=(spec,) * 5,
        scratch_shapes=scratch,
        compiler_params=pltpu.CompilerParams(
            collective_id=0, has_side_effects=True, vmem_limit_bytes=58 * 1024 * 1024
        ),
        cost_estimate=pl.CostEstimate(flops=8 * 10**9, bytes_accessed=10**7, transcendentals=0),
    )(inputs, rows_b, rows_c, log_decay, score_cotangent, out_weight)
    return pl.pallas_call(
        hand_on,
        out_shape=shapes,
        in_specs=[pl.BlockSpec(memory_space=pltpu.HBM)] * 5,
        out_specs=(spec,) * 3,
        scratch_shapes=[vm((512, 512), BF), vm((512, 1024), BF)]
        + [vm((512, 512), BF)] * 4
        + [dma((5,)), dma((3,))],
        cost_estimate=pl.CostEstimate(flops=0, bytes_accessed=4 * 2**20, transcendentals=0),
    )(*outs)


def solution(mesh):
    return jax.shard_map(
        local,
        mesh=mesh,
        in_specs=(
            P("seq", "head"),
            P("seq", None),
            P("seq", None),
            P("head", "seq"),
            P("seq", "head"),
            P("head", None),
        ),
        out_specs=(P("seq", "head"), P("seq", "head"), P("seq", "head")),
        check_vma=False,
    )
```
